128 devices in a mesh: seq: 64 (over z_hi, x, y, core), mp: 2 (over z_lo).
Axes of the slice: x: 4, y: 4, z: 4 (z_hi: 2, z_lo: 2; z = z_hi * 2 + z_lo), core: 2. Of those that a mesh axis runs over, the one named last changes fastest.
Arguments:
- clip_tokens: bfloat16 [512, 256, 768], P('seq'), may hold values from -6 to 6
- gain_spatial: float32 [768], replicated, may hold values from 0.5 to 1.5
- gain_temporal: float32 [768], replicated, may hold values from 0.5 to 1.5
- gain_mlp: float32 [768], replicated, may hold values from 0.5 to 1.5
- spatial_qkv: bfloat16 [768, 3, 768], P(None, None, 'mp'), may hold values from -0.21875 to 0.21875
- spatial_out: bfloat16 [768, 768], P('mp'), may hold values from -0.21875 to 0.21875
- temporal_qkv: bfloat16 [768, 3, 768], P(None, None, 'mp'), may hold values from -0.21875 to 0.21875
- temporal_out: bfloat16 [768, 768], P('mp'), may hold values from -0.21875 to 0.21875
- up_weight: bfloat16 [768, 3072], P(None, 'mp'), may hold values from -0.21875 to 0.21875
- down_weight: bfloat16 [3072, 768], P('mp'), may hold values from -0.109375 to 0.109375
Outputs:
- block_out: bfloat16 [512, 256, 768], P(('seq', 'mp'))
The draws below stay inside these ranges and needn't reach their ends.
All inputs are finite; a program needn't handle non-finite values.
Results may differ from the reference program's by a relative error of at most 0.019.
Values may be sent and summed in bfloat16 or wider, within the bound.
A program may use at most 128 MiB of HBM per device.

```python
import jax
import jax.numpy as jnp
from jax import lax

D = 768
HEAD_DIM = 64
FF = 3072
PATCHES = 256
FR_DEV = 8
FRAMES = 512
N_SEQ = 64


def block_levels(stream_key, shape, split, low, largest):
    level, own = 1.0, jax.random.fold_in(stream_key, 6)
    for position, blocks in split:
        steps = jnp.exp(jax.random.uniform(jax.random.fold_in(own, position), (blocks,), jnp.float32, low / len(split), largest / len(split)))
        level = level * jnp.repeat(steps, shape[position] // blocks).reshape([-1 if axis == position else 1 for axis in range(len(shape))])
    return level


def noise(stream_key, dims, deviation, bound, pieces=(), kind=jnp.bfloat16):
    factor_of = block_levels(stream_key, dims, pieces, -0.22, 0.18) if pieces else 1.0
    array = jax.random.normal(stream_key, dims, jnp.float32) * deviation * factor_of
    return jnp.minimum(jnp.maximum(array, -bound), bound).astype(kind)


def setup_inputs(seed: int = 0) -> dict:
    key_of = jax.random.split(jax.random.key(seed), 11)
    return {
        "clip_tokens": noise(key_of[0], (FRAMES, PATCHES, D), 1.0, 6.0, ((0, 64),)),
        "gain_spatial": jnp.clip(jax.random.uniform(key_of[1], (D,), jnp.float32, 0.5, 1.5), 0.5, 1.5),
        "gain_temporal": jnp.clip(jax.random.uniform(key_of[2], (D,), jnp.float32, 0.5, 1.5), 0.5, 1.5),
        "gain_mlp": jnp.clip(jax.random.uniform(key_of[3], (D,), jnp.float32, 0.5, 1.5), 0.5, 1.5),
        "spatial_qkv": noise(key_of[4], (D, 3, D), D ** -0.5, 0.21875, ((2, 2),)),
        "spatial_out": noise(key_of[5], (D, D), D ** -0.5, 0.21875, ((0, 2),)),
        "temporal_qkv": noise(key_of[6], (D, 3, D), D ** -0.5, 0.21875, ((2, 2),)),
        "temporal_out": noise(key_of[7], (D, D), D ** -0.5, 0.21875, ((0, 2),)),
        "up_weight": noise(key_of[8], (D, FF), D ** -0.5, 0.21875, ((1, 2),)),
        "down_weight": noise(key_of[9], (FF, D), FF ** -0.5, 0.109375, ((0, 2),)),
    }


def normalize(values, gain):
    values = values.astype(jnp.float32)
    center = values - lax.optimization_barrier(jnp.mean(values, axis=-1, keepdims=True))
    spread = lax.optimization_barrier(jnp.mean(center * center, axis=-1, keepdims=True))
    return (center * lax.rsqrt(spread + 1e-05) * gain).astype(jnp.bfloat16)

def attend(normed, w_qkv, w_out):
    batch, length, _ = normed.shape
    width = w_qkv.shape[2]
    heads = width // HEAD_DIM
    qkv = jnp.einsum('bld,dcw->blcw', normed.astype(jnp.float32), w_qkv.astype(jnp.float32)).astype(jnp.bfloat16)
    query = qkv[:, :, 0].reshape(batch, length, heads, HEAD_DIM).astype(jnp.float32)
    keys = qkv[:, :, 1].reshape(batch, length, heads, HEAD_DIM).astype(jnp.float32)
    vals = qkv[:, :, 2].reshape(batch, length, heads, HEAD_DIM).astype(jnp.float32)
    scores = jnp.einsum('bqhe,bkhe->bhqk', query, keys) * HEAD_DIM ** (-0.5)
    weights = jnp.exp(scores)
    weights = (weights / lax.optimization_barrier(jnp.sum(weights, axis=-1, keepdims=True))).astype(jnp.bfloat16)
    mixed = jnp.einsum('bhqk,bkhe->bqhe', weights.astype(jnp.float32), vals).astype(jnp.bfloat16)
    mixed = mixed.reshape(batch, length, width)
    return jnp.einsum('blw,wd->bld', mixed.astype(jnp.float32), w_out.astype(jnp.float32))

def reference(clip_tokens, gain_spatial, gain_temporal, gain_mlp, spatial_qkv, spatial_out, temporal_qkv, temporal_out, up_weight, down_weight):
    frame_blocks = clip_tokens.reshape(N_SEQ, FR_DEV, PATCHES, D)

    def spatial_block(block):
        mixed = attend(normalize(block, gain_spatial), spatial_qkv, spatial_out)
        return (block.astype(jnp.float32) + mixed).astype(jnp.bfloat16)
    spatial = lax.map(spatial_block, frame_blocks).reshape(FRAMES, PATCHES, D)
    position_blocks = jnp.swapaxes(spatial, 0, 1).reshape(PATCHES // 4, 4, FRAMES, D)

    def temporal_block(block):
        mixed = attend(normalize(block, gain_temporal), temporal_qkv, temporal_out)
        temporal = (block.astype(jnp.float32) + mixed).astype(jnp.bfloat16)
        normed = normalize(temporal, gain_mlp)
        up = jnp.einsum('bld,dh->blh', normed.astype(jnp.float32), up_weight.astype(jnp.float32))
        hidden = jax.nn.gelu(up, approximate=False).astype(jnp.bfloat16)
        down = jnp.einsum('blh,hd->bld', hidden.astype(jnp.float32), down_weight.astype(jnp.float32))
        return (temporal.astype(jnp.float32) + down).astype(jnp.bfloat16)
    result = lax.map(temporal_block, position_blocks).reshape(PATCHES, FRAMES, D)
    return jnp.swapaxes(result, 0, 1)
```

```python
import jax
import jax.numpy as jnp
from jax import lax
from jax.sharding import PartitionSpec as P

HEAD_DIM = 64


def normalize(values, gain):
    values = values.astype(jnp.float32)
    center = values - jnp.mean(values, axis=-1, keepdims=True)
    spread = jnp.mean(center * center, axis=-1, keepdims=True)
    return (center * lax.rsqrt(spread + 1e-05) * gain).astype(jnp.bfloat16)


def attend(normed, w_qkv, w_out):
    batch, length, _ = normed.shape
    width = w_qkv.shape[2]
    heads = width // HEAD_DIM
    qkv = jnp.einsum("bld,dcw->blcw", normed, w_qkv, preferred_element_type=jnp.float32).astype(
        jnp.bfloat16
    )
    query = qkv[:, :, 0].reshape(batch, length, heads, HEAD_DIM)
    keys = qkv[:, :, 1].reshape(batch, length, heads, HEAD_DIM)
    vals = qkv[:, :, 2].reshape(batch, length, heads, HEAD_DIM)
    scores = jnp.einsum(
        "bqhe,bkhe->bhqk", query, keys, preferred_element_type=jnp.float32
    ) * HEAD_DIM ** (-0.5)
    weights = jnp.exp(scores)
    weights = (weights / jnp.sum(weights, axis=-1, keepdims=True)).astype(jnp.bfloat16)
    mixed = jnp.einsum("bhqk,bkhe->bqhe", weights, vals, preferred_element_type=jnp.float32).astype(
        jnp.bfloat16
    )
    mixed = mixed.reshape(batch, length, width)
    return jnp.einsum("blw,wd->bld", mixed, w_out, preferred_element_type=jnp.float32)


def per_device(
    clip_tokens,
    gain_spatial,
    gain_temporal,
    gain_mlp,
    spatial_qkv,
    spatial_out,
    temporal_qkv,
    temporal_out,
    up_weight,
    down_weight,
):
    frame_count, patch_count, width = clip_tokens.shape
    model_count = lax.axis_size("mp")
    model_index = lax.axis_index("mp")
    half_frames = frame_count // model_count

    def whole(weight, axis):
        return lax.all_gather(weight, "mp", axis=axis, tiled=True)

    spatial_qkv, spatial_out = whole(spatial_qkv, 2), whole(spatial_out, 0)
    temporal_qkv, temporal_out = whole(temporal_qkv, 2), whole(temporal_out, 0)
    up_weight, down_weight = whole(up_weight, 1), whole(down_weight, 0)
    own = lax.dynamic_slice_in_dim(clip_tokens, model_index * half_frames, half_frames, 0)
    mixed = attend(normalize(own, gain_spatial), spatial_qkv, spatial_out)
    spatial = (own.astype(jnp.float32) + mixed).astype(jnp.bfloat16)
    positions = lax.all_to_all(spatial, ("seq", "mp"), split_axis=1, concat_axis=0, tiled=True)
    positions = jnp.swapaxes(positions, 0, 1)
    mixed = attend(normalize(positions, gain_temporal), temporal_qkv, temporal_out)
    temporal = (positions.astype(jnp.float32) + mixed).astype(jnp.bfloat16)
    up = jnp.einsum(
        "bfd,dh->bfh", normalize(temporal, gain_mlp), up_weight, preferred_element_type=jnp.float32
    )
    hidden = jax.nn.gelu(up, approximate=False).astype(jnp.bfloat16)
    down = jnp.einsum("bfh,hd->bfd", hidden, down_weight, preferred_element_type=jnp.float32)
    finished = jnp.swapaxes((temporal.astype(jnp.float32) + down).astype(jnp.bfloat16), 0, 1)
    return lax.all_to_all(finished, ("seq", "mp"), split_axis=0, concat_axis=1, tiled=True)


def solution(mesh):
    return jax.shard_map(
        per_device,
        mesh=mesh,
        in_specs=(
            P("seq", None, None),
            P(),
            P(),
            P(),
            P(None, None, "mp"),
            P("mp", None),
            P(None, None, "mp"),
            P("mp", None),
            P(None, "mp"),
            P("mp", None),
        ),
        out_specs=P(("seq", "mp"), None, None),
        check_vma=False,
    )
```

```python
import functools
import math

import jax
import jax.numpy as jnp
from jax import lax
from jax.experimental import pallas as pl
from jax.experimental.pallas import tpu as pltpu
from jax.sharding import PartitionSpec as P

MESH = pl.DeviceIdType.MESH
F32, BF16 = jnp.float32, jnp.bfloat16
HEAD_DIM = 64
D = 768
HALF = 384
TOKENS = 256
DEVICES = 128
GROUP = 32
Q_SCALE = math.log2(math.e) * HEAD_DIM**-0.5
ROWS = (768, 384, 768, 384, 768, 1536)
STACKED = (False, True, False, True, False, True)


def dot(a, b):
    return jnp.dot(a, b, preferred_element_type=F32)


def layer_norm(values, gain):
    values = values.astype(F32)
    center = values - jnp.mean(values, axis=-1, keepdims=True)
    spread = jnp.mean(center * center, axis=-1, keepdims=True)
    return (center * lax.rsqrt(spread + 1e-05) * gain).astype(BF16)


def attend_pair(query, keys, vals):
    first = lax.broadcasted_iota(jnp.int32, (1, 128), 1) < HEAD_DIM
    zero = jnp.zeros_like(query)
    one = jnp.ones_like(vals)
    outs = []
    for mine in (first, jnp.logical_not(first)):
        scores = lax.dot_general(
            jnp.where(mine, query, zero), keys, (((1,), (1,)), ((), ())), preferred_element_type=F32
        )
        weights = jnp.exp2(scores).astype(BF16)
        filled = jnp.where(mine, vals, one)
        both = jnp.concatenate([filled * BF16(2.0**-8), filled * BF16(2.0**24)], axis=1)
        outs.append(dot(weights, both))
    out_a, out_b = outs
    low_top, low_sum = jnp.where(first, out_a[:, :128], out_b[:, :128]), jnp.where(
        first, out_b[:, :128], out_a[:, :128]
    )
    high_top, high_sum = jnp.where(first, out_a[:, 128:], out_b[:, 128:]), jnp.where(
        first, out_b[:, 128:], out_a[:, 128:]
    )
    low_sum = pltpu.roll(low_sum, HEAD_DIM, 1)
    high_sum = pltpu.roll(high_sum, HEAD_DIM, 1)
    large = low_sum > 2.0**-8
    return (jnp.where(large, low_top, high_top) / jnp.where(large, low_sum, high_sum)).astype(BF16)


def gelu(value):
    return 0.5 * value * (1.0 + lax.erf(value * 0.5**0.5))


def bits(index, *fields):
    total = jnp.zeros_like(index)
    for shift, width, to in fields:
        total = total + (((index >> shift) & ((1 << width) - 1)) << to)
    return total


def one_hot(*fields):
    row = lax.broadcasted_iota(jnp.int32, (512, 512), 0)
    column = lax.broadcasted_iota(jnp.int32, (512, 512), 1)
    return jnp.where(bits(row, *fields) == column, 1.0, 0.0).astype(BF16)


def kernel(
    clip, gain_s, gain_t, gain_m, w0, w1, w2, w3, w4, w5, out,
    x, normed, qkv_s, qkv_t, mixed, positions,
    send1, recv1, send2, recv2, perm,
    f0, f1, f2, f3, f4, f5,
    x_sem, own_sem, z_send, z_recv, core_send, core_recv, round_sem,
    a_send, a_recv, b_send, b_recv,
):
    s, m = lax.axis_index("seq"), lax.axis_index("mp")
    me = s * 2 + m
    group, place = me // GROUP, lax.rem(me, GROUP)
    z_hi, core = s // 32, lax.rem(s, 2)
    owned = (w0, w1, w2, w3, w4, w5)
    full = (f0, f1, f2, f3, f4, f5)

    def part(k, half, start, rows):
        if STACKED[k]:
            return full[k].at[pl.ds(pl.multiple_of(half * ROWS[k] + start, 16), rows)]
        return full[k].at[half, pl.ds(pl.multiple_of(start, 16), rows)]

    def flip(bit):
        return me + bit * (1 - 2 * lax.rem(me // bit, 2))

    def device(index):
        return (index // 2, lax.rem(index, 2))

    def load(k):
        return pltpu.make_async_copy(owned[k], part(k, m, 0, ROWS[k]), own_sem.at[k])

    def z_start(k):
        rows = ROWS[k] // 4
        start = (z_hi * 2 + core) * rows
        for other in range(2):
            pltpu.make_async_remote_copy(
                src_ref=owned[k].at[pl.ds(pl.multiple_of(start, 16), rows)],
                dst_ref=part(k, m, start, rows),
                send_sem=z_send.at[k],
                recv_sem=z_recv.at[k, z_hi],
                device_id=(other * 32 + lax.rem(s, 32), 1 - m),
                device_id_type=MESH,
            ).start()

    def z_forward(k):
        rows = ROWS[k] // 4
        for source in range(2):
            piece = part(k, 1 - m, (source * 2 + core) * rows, rows)
            pltpu.make_async_copy(piece, piece, z_recv.at[k, source]).wait()
            pltpu.make_async_remote_copy(
                src_ref=piece,
                dst_ref=piece,
                send_sem=core_send.at[k],
                recv_sem=core_recv.at[k],
                device_id=device(flip(2)),
                device_id_type=MESH,
            ).start()

    def half_bytes(k, sem):
        block = part(k, 0, 0, ROWS[k] // 2)
        pltpu.make_async_copy(block, block, sem.at[k]).wait()

    def z_finish(k):
        half_bytes(k, core_recv)

    def exchange(b, to, send, recv, send_sem, recv_sem):
        @pl.when(b == 0)
        def _():
            own = pl.ds(pl.multiple_of(me * 16, 16), 16)
            pltpu.make_async_copy(send.at[own], recv.at[own], recv_sem.at[group]).start()

        def step(i, carry):
            dest = to * GROUP + lax.rem(i + place, GROUP)
            pltpu.make_async_remote_copy(
                src_ref=send.at[pl.ds(pl.multiple_of(dest * 16, 16), 16)],
                dst_ref=recv.at[pl.ds(pl.multiple_of(me * 16, 16), 16)],
                send_sem=send_sem,
                recv_sem=recv_sem.at[group],
                device_id=device(dest),
                device_id_type=MESH,
            ).start()
            return carry

        lax.fori_loop(jnp.where(b == 0, 1, 0), GROUP, step, 0)

    def arrived(recv, recv_sem, source):
        block = recv.at[pl.ds(pl.multiple_of(source * 512, 512), 512)]
        pltpu.make_async_copy(block, block, recv_sem.at[source]).wait()
        return block[...]

    barrier = pltpu.get_barrier_semaphore()
    for bit in (1, 2, 4, 8, 16, 32, 64):
        pl.semaphore_signal(barrier, inc=1, device_id=device(flip(bit)), device_id_type=MESH)
    pl.semaphore_signal(
        barrier, inc=1, device_id=(lax.rem(s + 32, 64), 1 - m), device_id_type=MESH
    )
    own_frames = pltpu.make_async_copy(clip.at[pl.ds(m * 4, 4)], x, x_sem)
    own_frames.start()
    for k in range(6):
        load(k).start()
    perm[0] = one_hot((4, 5, 1), (3, 1, 8), (2, 1, 0), (0, 2, 6))
    perm[1] = one_hot((8, 1, 3), (7, 1, 2), (2, 5, 4), (0, 2, 0))
    perm[2] = one_hot((4, 5, 2), (3, 1, 8), (2, 1, 7), (0, 2, 0))
    perm[3] = one_hot((8, 1, 3), (6, 2, 0), (1, 5, 4), (0, 1, 2))
    own_frames.wait()

    @pl.loop(0, 4)
    def _(f):
        normed[pl.ds(pl.multiple_of(f * TOKENS, TOKENS), TOKENS)] = layer_norm(x[f], gain_s[...])

    pl.semaphore_wait(barrier, 8)
    z_start(0)
    z_start(1)

    columns = lax.broadcasted_iota(jnp.int32, (1, 3 * HALF), 1)
    scale = jnp.where(columns < HALF, Q_SCALE, 1.0).astype(F32)

    def spatial_heads(half):
        @pl.loop(0, 4)
        def _(f):
            rows = pl.ds(pl.multiple_of(f * TOKENS, TOKENS), TOKENS)
            qkv_s[rows] = (dot(normed[rows], f0[half]) * scale).astype(BF16)

        @pl.loop(0, 4)
        def _(f):
            rows = pl.ds(pl.multiple_of(f * TOKENS, TOKENS), TOKENS)
            for pair in range(3):
                c = pair * 128
                mixed[rows, pl.ds(pl.multiple_of(half * HALF + c, 128), 128)] = attend_pair(
                    qkv_s[rows, c : c + 128],
                    qkv_s[rows, HALF + c : HALF + c + 128],
                    qkv_s[rows, 2 * HALF + c : 2 * HALF + c + 128],
                )

    load(0).wait()
    spatial_heads(m)
    for r in range(7):
        pl.semaphore_signal(
            round_sem.at[r], inc=1, device_id=device(flip(1 << r)), device_id_type=MESH
        )
        pl.semaphore_wait(round_sem.at[r], 1)
    z_forward(0)
    z_forward(1)
    z_start(2)
    z_start(3)
    z_finish(0)
    spatial_heads(1 - m)
    load(1).wait()
    z_finish(1)

    @pl.loop(0, 4)
    def _(f):
        rows = pl.ds(pl.multiple_of(f * TOKENS, TOKENS), TOKENS)
        x[f] = (x[f].astype(F32) + dot(mixed[rows], f1[...])).astype(BF16)

    @pl.loop(0, 4)
    def _(b):
        to = lax.rem(group + b, 4)
        rows = pl.ds(pl.multiple_of(to * 64, 64), 64)
        block = jnp.concatenate(
            [x[f, rows, h * HALF : (h + 1) * HALF] for h in range(2) for f in range(4)], axis=0
        )
        send1[pl.ds(pl.multiple_of(to * 512, 512), 512)] = dot(perm[0], block).astype(BF16)
        exchange(b, to, send1, recv1, a_send, a_recv)

    z_start(4)
    z_start(5)
    z_forward(2)
    z_forward(3)
    load(2).wait()
    z_finish(2)

    @pl.loop(0, 4)
    def _(b):
        source = lax.rem(group + 4 - b, 4)
        block = dot(perm[1], arrived(recv1, a_recv, source)).astype(BF16)
        tokens = jnp.concatenate([block[:TOKENS], block[TOKENS:]], axis=1)
        normal = layer_norm(tokens, gain_t[...])
        for p in range(2):
            rows = pl.ds(pl.multiple_of(p * 512 + b * 128, 128), 128)
            positions[rows] = tokens[p * 128 : (p + 1) * 128]
        for half in range(2):
            made = (dot(normal, f2[half]) * scale).astype(BF16)
            for p in range(2):
                qkv_t[half, pl.ds(pl.multiple_of(p * 512 + b * 128, 128), 128)] = made[
                    p * 128 : (p + 1) * 128
                ]

    for p in range(2):

        @pl.loop(0, 4)
        def _(t):
            half = t // 2
            every = slice(p * 512, (p + 1) * 512)
            rows = pl.ds(pl.multiple_of(p * 512 + lax.rem(t, 2) * TOKENS, TOKENS), TOKENS)
            for pair in range(3):
                c = pair * 128
                mixed[rows, pl.ds(pl.multiple_of(half * HALF + c, 128), 128)] = attend_pair(
                    qkv_t[half, rows, c : c + 128],
                    qkv_t[half, every, HALF + c : HALF + c + 128],
                    qkv_t[half, every, 2 * HALF + c : 2 * HALF + c + 128],
                )

        z_forward(4 + p)

    load(3).wait()
    z_finish(3)
    load(4).wait()
    z_finish(4)
    load(5).wait()
    z_finish(5)

    @pl.loop(0, 4)
    def _(b):
        rows = [pl.ds(pl.multiple_of(p * 512 + b * 128, 128), 128) for p in range(2)]
        total = dot(jnp.concatenate([mixed[r] for r in rows], axis=0), f3[...])
        tokens = jnp.concatenate([positions[r] for r in rows], axis=0)
        tokens = (tokens.astype(F32) + total).astype(BF16)
        normal = layer_norm(tokens, gain_m[...])
        total = tokens.astype(F32)
        for j in range(4):
            up = dot(normal, f4[j // 2, :, (j % 2) * D : (j % 2 + 1) * D])
            total = total + dot(gelu(up).astype(BF16), f5[j * D : (j + 1) * D])
        done = total.astype(BF16)
        block = jnp.concatenate([done[:, :HALF], done[:, HALF:]], axis=0)
        to = lax.rem(group + 4 - b, 4)
        send2[pl.ds(pl.multiple_of(to * 512, 512), 512)] = dot(perm[2], block).astype(BF16)
        exchange(b, to, send2, recv2, b_send, b_recv)

    @pl.loop(0, 4)
    def _(b):
        source = lax.rem(group + b, 4)
        block = dot(perm[3], arrived(recv2, b_recv, source)).astype(BF16)
        rows = pl.ds(pl.multiple_of(source * 64, 64), 64)
        for h in range(2):
            for f in range(4):
                at = h * TOKENS + f * 64
                out[f, rows, h * HALF : (h + 1) * HALF] = block[at : at + 64]

    for send, sem in ((send1, a_send), (send2, b_send)):
        sent = send.at[pl.ds(0, (DEVICES - 1) * 16)]
        pltpu.make_async_copy(sent, sent, sem).wait()
    for k in range(6):
        half_bytes(k, z_send)
        half_bytes(k, core_send)


def per_device(clip, gain_s, gain_t, gain_m, w0, w1, w2, w3, w4, w5):
    w0, w2 = w0.reshape(D, 3 * HALF), w2.reshape(D, 3 * HALF)
    gains = [g.reshape(1, D) for g in (gain_s, gain_t, gain_m)]
    vmem, anywhere = pl.BlockSpec(memory_space=pltpu.VMEM), pl.BlockSpec(memory_space=pl.ANY)
    dma = pltpu.SemaphoreType.DMA
    return pl.pallas_call(
        kernel,
        out_shape=jax.ShapeDtypeStruct((4, 256, D), BF16),
        in_specs=[anywhere, vmem, vmem, vmem] + [anywhere] * 6,
        out_specs=vmem,
        scratch_shapes=[
            pltpu.VMEM((4, 256, D), BF16),
            pltpu.VMEM((1024, D), BF16),
            pltpu.VMEM((1024, 3 * HALF), BF16),
            pltpu.VMEM((2, 1024, 3 * HALF), BF16),
            pltpu.VMEM((1024, D), BF16),
            pltpu.VMEM((1024, D), BF16),
            pltpu.VMEM((2048, HALF), BF16),
            pltpu.VMEM((2048, HALF), BF16),
            pltpu.VMEM((2048, HALF), BF16),
            pltpu.VMEM((2048, HALF), BF16),
            pltpu.VMEM((4, 512, 512), BF16),
            pltpu.VMEM((2, D, 3 * HALF), BF16),
            pltpu.VMEM((D, D), BF16),
            pltpu.VMEM((2, D, 3 * HALF), BF16),
            pltpu.VMEM((D, D), BF16),
            pltpu.VMEM((2, D, 1536), BF16),
            pltpu.VMEM((3072, D), BF16),
            dma,
            dma((6,)),
            dma((6,)),
            dma((6, 2)),
            dma((6,)),
            dma((6,)),
            pltpu.SemaphoreType.REGULAR((7,)),
            dma,
            dma((4,)),
            dma,
            dma((4,)),
        ],
        compiler_params=pltpu.CompilerParams(
            collective_id=0, has_side_effects=True, vmem_limit_bytes=60 << 20
        ),
        cost_estimate=pl.CostEstimate(
            flops=22 * 10**9, bytes_accessed=13 * 10**6, transcendentals=12 * 10**6
        ),
    )(clip, *gains, w0, w1, w2, w3, w4, w5)


def solution(mesh):
    return jax.shard_map(
        per_device,
        mesh=mesh,
        in_specs=(
            P("seq", None, None),
            P(),
            P(),
            P(),
            P(None, None, "mp"),
            P("mp", None),
            P(None, None, "mp"),
            P("mp", None),
            P(None, "mp"),
            P("mp", None),
        ),
        out_specs=P(("seq", "mp"), None, None),
        check_vma=False,
    )
```

```python
import functools
import math

import jax
import jax.numpy as jnp
from jax import lax
from jax.experimental import pallas as pl
from jax.experimental.pallas import tpu as pltpu
from jax.sharding import PartitionSpec as P

MESH = pl.DeviceIdType.MESH
F32, BF16 = jnp.float32, jnp.bfloat16
HEAD_DIM = 64
D = 768
HALF = 384
TOKENS = 256
DEVICES = 128
GROUP = 32
Q_SCALE = math.log2(math.e) * HEAD_DIM**-0.5
ROWS = (768, 384, 768, 384, 768, 1536)
STACKED = (False, True, False, True, False, True)


def dot(a, b):
    return jnp.dot(a, b, preferred_element_type=F32)


def layer_norm(values, gain):
    values = values.astype(F32)
    center = values - jnp.mean(values, axis=-1, keepdims=True)
    spread = jnp.mean(center * center, axis=-1, keepdims=True)
    return (center * lax.rsqrt(spread + 1e-05) * gain).astype(BF16)


def attend_pair(query, keys, vals):
    first = lax.broadcasted_iota(jnp.int32, (1, 128), 1) < HEAD_DIM
    zero = jnp.zeros_like(query)
    one = jnp.ones_like(vals)
    outs = []
    for mine in (first, jnp.logical_not(first)):
        scores = lax.dot_general(
            jnp.where(mine, query, zero), keys, (((1,), (1,)), ((), ())), preferred_element_type=F32
        )
        weights = jnp.exp2(scores).astype(BF16)
        filled = jnp.where(mine, vals, one)
        both = jnp.concatenate([filled * BF16(2.0**-8), filled * BF16(2.0**24)], axis=1)
        outs.append(dot(weights, both))
    out_a, out_b = outs
    low_top, low_sum = jnp.where(first, out_a[:, :128], out_b[:, :128]), jnp.where(
        first, out_b[:, :128], out_a[:, :128]
    )
    high_top, high_sum = jnp.where(first, out_a[:, 128:], out_b[:, 128:]), jnp.where(
        first, out_b[:, 128:], out_a[:, 128:]
    )
    low_sum = pltpu.roll(low_sum, HEAD_DIM, 1)
    high_sum = pltpu.roll(high_sum, HEAD_DIM, 1)
    large = low_sum > 2.0**-8
    return (jnp.where(large, low_top, high_top) / jnp.where(large, low_sum, high_sum)).astype(BF16)


def gelu(value):
    return 0.5 * value * (1.0 + lax.erf(value * 0.5**0.5))


def bits(index, *fields):
    total = jnp.zeros_like(index)
    for shift, width, to in fields:
        total = total + (((index >> shift) & ((1 << width) - 1)) << to)
    return total


def one_hot(*fields):
    row = lax.broadcasted_iota(jnp.int32, (512, 512), 0)
    column = lax.broadcasted_iota(jnp.int32, (512, 512), 1)
    return jnp.where(bits(row, *fields) == column, 1.0, 0.0).astype(BF16)


def kernel(
    clip, gain_s, gain_t, gain_m, w0, w1, w2, w3, w4, w5, out,
    x, normed, qkv_s, qkv_t, mixed, positions,
    send1, recv1, send2, recv2, perm,
    f0, f1, f2, f3, f4, f5,
    x_sem, own_sem, z_send, z_recv, ring_send, ring_recv, far_recv, core_send, core_recv, round_sem,
    a_send, a_recv, b_send, b_recv,
):
    s, m = lax.axis_index("seq"), lax.axis_index("mp")
    me = s * 2 + m
    group, place = me // GROUP, lax.rem(me, GROUP)
    z_hi, core = s // 32, lax.rem(s, 2)
    x_at, y_at = lax.rem(s // 8, 4), lax.rem(s // 2, 4)
    ring_place = x_at * (1 - core) + y_at * core
    above = (lax.rem(z_hi + m, 2) * 32 + lax.rem(s, 32), 1 - m)
    below = (lax.rem(z_hi + 1 - m, 2) * 32 + lax.rem(s, 32), 1 - m)
    owned = (w0, w1, w2, w3, w4, w5)
    full = (f0, f1, f2, f3, f4, f5)

    def part(k, half, start, rows):
        if STACKED[k]:
            return full[k].at[pl.ds(pl.multiple_of(half * ROWS[k] + start, 16), rows)]
        return full[k].at[half, pl.ds(pl.multiple_of(start, 16), rows)]

    def flip(bit):
        return me + bit * (1 - 2 * lax.rem(me // bit, 2))

    def device(index):
        return (index // 2, lax.rem(index, 2))

    def copy(ref, send_sem, recv_sem, to):
        pltpu.make_async_remote_copy(
            src_ref=ref, dst_ref=ref, send_sem=send_sem, recv_sem=recv_sem, device_id=to, device_id_type=MESH
        ).start()

    def landed(ref, sem):
        pltpu.make_async_copy(ref, ref, sem).wait()

    def load(k):
        if k in (0, 2):
            for c in range(3):
                columns = full[k].at[m, :, c * HALF : (c + 1) * HALF]
                pltpu.make_async_copy(owned[k].at[c], columns, own_sem.at[k]).start()
        else:
            pltpu.make_async_copy(owned[k], part(k, m, 0, ROWS[k]), own_sem.at[k]).start()

    def loaded(k):
        landed(part(k, m, 0, ROWS[k]), own_sem.at[k])

    def quarter(k, half, step, sub=None):
        rows = ROWS[k] // 8
        start = core * (ROWS[k] // 2) + lax.rem(ring_place + step + 4, 4) * rows
        if sub is None:
            return part(k, half, start, rows)
        if STACKED[k]:
            return part(k, half, start, rows).at[:, sub * HALF : (sub + 1) * HALF]
        return part(k, half, start + sub * (rows // 2), rows // 2)

    def ring(step):
        to_x, to_y = lax.rem(x_at + step * (1 - core) + 4, 4), lax.rem(y_at + step * core + 4, 4)
        return (z_hi * 32 + to_x * 8 + to_y * 2 + core, m)

    def fetch_z(k):
        loaded(k)
        for sub in range(2):
            copy(quarter(k, m, 0, sub), z_send.at[k], z_recv.at[k, sub], above if sub == 0 else below)

    def fetch_ring(k):
        for sub in range(2):
            landed(quarter(k, 1 - m, 0, sub), z_recv.at[k, sub])
        for way, step in enumerate((1, -1)):
            copy(quarter(k, 1 - m, 0), ring_send.at[k], ring_recv.at[k, way], ring(step))
        copy(quarter(k, 1 - m, 0), core_send.at[k], core_recv.at[k], device(flip(2)))

    def fetch_far(k):
        for way, step in enumerate((1, -1)):
            landed(quarter(k, 1 - m, -step), ring_recv.at[k, way])
            copy(quarter(k, 1 - m, -step, way), ring_send.at[k], far_recv.at[k, way], ring(step))
            copy(quarter(k, 1 - m, -step), core_send.at[k], core_recv.at[k], device(flip(2)))

    def fetch_last(k):
        for way in range(2):
            landed(quarter(k, 1 - m, 2, way), far_recv.at[k, way])
        copy(quarter(k, 1 - m, 2), core_send.at[k], core_recv.at[k], device(flip(2)))

    def fetched(k):
        landed(part(k, 0, 0, ROWS[k] // 2), core_recv.at[k])

    def exchange(b, to, send, recv, send_sem, recv_sem):
        @pl.when(b == 0)
        def _():
            own = pl.ds(pl.multiple_of(me * 16, 16), 16)
            pltpu.make_async_copy(send.at[own], recv.at[own], recv_sem.at[group]).start()

        def step(i, carry):
            dest = to * GROUP + lax.rem(i + place, GROUP)
            pltpu.make_async_remote_copy(
                src_ref=send.at[pl.ds(pl.multiple_of(dest * 16, 16), 16)],
                dst_ref=recv.at[pl.ds(pl.multiple_of(me * 16, 16), 16)],
                send_sem=send_sem,
                recv_sem=recv_sem.at[group],
                device_id=device(dest),
                device_id_type=MESH,
            ).start()
            return carry

        lax.fori_loop(jnp.where(b == 0, 1, 0), GROUP, step, 0)

    def arrived(recv, recv_sem, source):
        block = recv.at[pl.ds(pl.multiple_of(source * 512, 512), 512)]
        pltpu.make_async_copy(block, block, recv_sem.at[source]).wait()
        return block[...]

    barrier = pltpu.get_barrier_semaphore()
    greeted = [device(flip(bit)) for bit in (2, 8, 32, 64)] + [above, below]
    for step in (1, 3):
        greeted.append((z_hi * 32 + lax.rem(x_at + step, 4) * 8 + y_at * 2 + core, m))
        greeted.append((z_hi * 32 + x_at * 8 + lax.rem(y_at + step, 4) * 2 + core, m))
    for other in greeted:
        pl.semaphore_signal(barrier, inc=1, device_id=other, device_id_type=MESH)
    own_frames = pltpu.make_async_copy(clip.at[pl.ds(m * 4, 4)], x, x_sem)
    own_frames.start()
    for k in range(6):
        load(k)
    perm[0] = one_hot((4, 5, 1), (3, 1, 8), (2, 1, 0), (0, 2, 6))
    perm[1] = one_hot((8, 1, 3), (7, 1, 2), (2, 5, 4), (0, 2, 0))
    perm[2] = one_hot((4, 5, 2), (3, 1, 8), (2, 1, 7), (0, 2, 0))
    perm[3] = one_hot((8, 1, 3), (6, 2, 0), (1, 5, 4), (0, 1, 2))
    own_frames.wait()

    @pl.loop(0, 4)
    def _(f):
        normed[pl.ds(pl.multiple_of(f * TOKENS, TOKENS), TOKENS)] = layer_norm(x[f], gain_s[...].reshape(1, D))

    pl.semaphore_wait(barrier, len(greeted))
    fetch_z(0)
    fetch_z(1)

    columns = lax.broadcasted_iota(jnp.int32, (1, 3 * HALF), 1)
    scale = jnp.where(columns < HALF, Q_SCALE, 1.0).astype(F32)

    def spatial_heads(half, after_qkv, beside):
        @pl.loop(0, 4)
        def _(f):
            rows = pl.ds(pl.multiple_of(f * TOKENS, TOKENS), TOKENS)
            qkv_s[rows] = (dot(normed[rows], f0[half]) * scale).astype(BF16)

        after_qkv()

        @pl.loop(0, 4)
        def _(f):
            for turn, service in beside.items():
                pl.when(f == turn)(service)
            rows = pl.ds(pl.multiple_of(f * TOKENS, TOKENS), TOKENS)
            for pair in range(3):
                c = pair * 128
                mixed[rows, pl.ds(pl.multiple_of(half * HALF + c, 128), 128)] = attend_pair(
                    qkv_s[rows, c : c + 128],
                    qkv_s[rows, HALF + c : HALF + c + 128],
                    qkv_s[rows, 2 * HALF + c : 2 * HALF + c + 128],
                )

    def rounds(low, high):
        for r in range(low, high):
            pl.semaphore_signal(
                round_sem.at[r], inc=1, device_id=device(flip((16, 32, 4, 8, 2, 1, 64)[r])), device_id_type=MESH
            )
            pl.semaphore_wait(round_sem.at[r], 1)

    def service_a():
        fetch_ring(0)
        fetch_ring(1)
        fetch_z(2)
        fetch_z(3)
        rounds(0, 2)

    def service_b():
        fetch_far(0)
        fetch_far(1)
        fetch_z(4)
        fetch_z(5)
        rounds(2, 4)

    def service_c():
        fetch_ring(2)
        fetch_ring(3)
        rounds(4, 7)

    def service_d():
        fetch_ring(4)
        fetch_ring(5)

    def service_e():
        fetch_far(2)
        fetch_far(3)

    spatial_heads(m, service_a, {2: service_b})
    fetch_last(0)
    fetch_last(1)
    service_c()
    fetched(0)
    spatial_heads(1 - m, service_d, {2: service_e})
    fetched(1)

    @pl.loop(0, 4)
    def _(f):
        rows = pl.ds(pl.multiple_of(f * TOKENS, TOKENS), TOKENS)
        x[f] = (x[f].astype(F32) + dot(mixed[rows], f1[...])).astype(BF16)

    @pl.loop(0, 4)
    def _(b):
        to = lax.rem(group + b, 4)
        rows = pl.ds(pl.multiple_of(to * 64, 64), 64)
        block = jnp.concatenate(
            [x[f, rows, h * HALF : (h + 1) * HALF] for h in range(2) for f in range(4)], axis=0
        )
        send1[pl.ds(pl.multiple_of(to * 512, 512), 512)] = dot(perm[0], block).astype(BF16)
        exchange(b, to, send1, recv1, a_send, a_recv)

    fetch_last(2)
    fetch_last(3)
    fetch_far(4)
    fetch_far(5)
    fetched(2)

    @pl.loop(0, 4)
    def _(b):
        source = lax.rem(group + 4 - b, 4)
        block = dot(perm[1], arrived(recv1, a_recv, source)).astype(BF16)
        tokens = jnp.concatenate([block[:TOKENS], block[TOKENS:]], axis=1)
        normal = layer_norm(tokens, gain_t[...].reshape(1, D))
        for p in range(2):
            rows = pl.ds(pl.multiple_of(p * 512 + b * 128, 128), 128)
            positions[rows] = tokens[p * 128 : (p + 1) * 128]
        for half in range(2):
            made = (dot(normal, f2[half]) * scale).astype(BF16)
            for p in range(2):
                qkv_t[half, pl.ds(pl.multiple_of(p * 512 + b * 128, 128), 128)] = made[
                    p * 128 : (p + 1) * 128
                ]

    for p in range(2):

        @pl.loop(0, 4)
        def _(t):
            half = t // 2
            every = slice(p * 512, (p + 1) * 512)
            rows = pl.ds(pl.multiple_of(p * 512 + lax.rem(t, 2) * TOKENS, TOKENS), TOKENS)
            for pair in range(3):
                c = pair * 128
                mixed[rows, pl.ds(pl.multiple_of(half * HALF + c, 128), 128)] = attend_pair(
                    qkv_t[half, rows, c : c + 128],
                    qkv_t[half, every, HALF + c : HALF + c + 128],
                    qkv_t[half, every, 2 * HALF + c : 2 * HALF + c + 128],
                )

        fetch_last(4 + p)

    fetched(3)
    fetched(4)
    fetched(5)

    @pl.loop(0, 4)
    def _(b):
        rows = [pl.ds(pl.multiple_of(p * 512 + b * 128, 128), 128) for p in range(2)]
        total = dot(jnp.concatenate([mixed[r] for r in rows], axis=0), f3[...])
        tokens = jnp.concatenate([positions[r] for r in rows], axis=0)
        tokens = (tokens.astype(F32) + total).astype(BF16)
        normal = layer_norm(tokens, gain_m[...].reshape(1, D))
        total = tokens.astype(F32)
        for j in range(4):
            up = dot(normal, f4[j // 2, :, (j % 2) * D : (j % 2 + 1) * D])
            total = total + dot(gelu(up).astype(BF16), f5[j * D : (j + 1) * D])
        done = total.astype(BF16)
        block = jnp.concatenate([done[:, :HALF], done[:, HALF:]], axis=0)
        to = lax.rem(group + 4 - b, 4)
        send2[pl.ds(pl.multiple_of(to * 512, 512), 512)] = dot(perm[2], block).astype(BF16)
        exchange(b, to, send2, recv2, b_send, b_recv)

    @pl.loop(0, 4)
    def _(b):
        source = lax.rem(group + b, 4)
        block = dot(perm[3], arrived(recv2, b_recv, source)).astype(BF16)
        rows = pl.ds(pl.multiple_of(source * 64, 64), 64)
        for h in range(2):
            for f in range(4):
                at = h * TOKENS + f * 64
                out[f, rows, h * HALF : (h + 1) * HALF] = block[at : at + 64]

    for send, sem in ((send1, a_send), (send2, b_send)):
        sent = send.at[pl.ds(0, (DEVICES - 1) * 16)]
        pltpu.make_async_copy(sent, sent, sem).wait()
    for k in range(6):
        landed(part(k, 0, 0, ROWS[k] // 8), z_send.at[k])
        landed(part(k, 0, 0, ROWS[k] // 8 * 3), ring_send.at[k])
        landed(part(k, 0, 0, ROWS[k] // 2), core_send.at[k])


def per_device(clip, gain_s, gain_t, gain_m, w0, w1, w2, w3, w4, w5):
    w0, w2 = jnp.swapaxes(w0, 0, 1), jnp.swapaxes(w2, 0, 1)
    vmem, anywhere = pl.BlockSpec(memory_space=pltpu.VMEM), pl.BlockSpec(memory_space=pl.ANY)
    dma = pltpu.SemaphoreType.DMA
    return pl.pallas_call(
        kernel,
        out_shape=jax.ShapeDtypeStruct((4, 256, D), BF16),
        in_specs=[anywhere, vmem, vmem, vmem] + [anywhere] * 6,
        out_specs=vmem,
        scratch_shapes=[
            pltpu.VMEM((4, 256, D), BF16),
            pltpu.VMEM((1024, D), BF16),
            pltpu.VMEM((1024, 3 * HALF), BF16),
            pltpu.VMEM((2, 1024, 3 * HALF), BF16),
            pltpu.VMEM((1024, D), BF16),
            pltpu.VMEM((1024, D), BF16),
            pltpu.VMEM((2048, HALF), BF16),
            pltpu.VMEM((2048, HALF), BF16),
            pltpu.VMEM((2048, HALF), BF16),
            pltpu.VMEM((2048, HALF), BF16),
            pltpu.VMEM((4, 512, 512), BF16),
            pltpu.VMEM((2, D, 3 * HALF), BF16),
            pltpu.VMEM((D, D), BF16),
            pltpu.VMEM((2, D, 3 * HALF), BF16),
            pltpu.VMEM((D, D), BF16),
            pltpu.VMEM((2, D, 1536), BF16),
            pltpu.VMEM((3072, D), BF16),
            dma,
            dma((6,)),
            dma((6,)),
            dma((6, 2)),
            dma((6,)),
            dma((6, 2)),
            dma((6, 2)),
            dma((6,)),
            dma((6,)),
            pltpu.SemaphoreType.REGULAR((7,)),
            dma,
            dma((4,)),
            dma,
            dma((4,)),
        ],
        compiler_params=pltpu.CompilerParams(
            collective_id=0, has_side_effects=True, vmem_limit_bytes=60 << 20
        ),
        cost_estimate=pl.CostEstimate(
            flops=22 * 10**9, bytes_accessed=13 * 10**6, transcendentals=12 * 10**6
        ),
    )(clip, gain_s, gain_t, gain_m, w0, w1, w2, w3, w4, w5)


def solution(mesh):
    return jax.shard_map(
        per_device,
        mesh=mesh,
        in_specs=(
            P("seq", None, None),
            P(),
            P(),
            P(),
            P(None, None, "mp"),
            P("mp", None),
            P(None, None, "mp"),
            P("mp", None),
            P(None, "mp"),
            P("mp", None),
        ),
        out_specs=P(("seq", "mp"), None, None),
        check_vma=False,
    )
```

```python
import functools
import math

import jax
import jax.numpy as jnp
from jax import lax
from jax.experimental import pallas as pl
from jax.experimental.pallas import tpu as pltpu
from jax.sharding import PartitionSpec as P

MESH = pl.DeviceIdType.MESH
F32, BF16 = jnp.float32, jnp.bfloat16
HEAD_DIM = 64
D = 768
HALF = 384
TOKENS = 256
CHIPS = 64
PACKED = 16 * 24
GROUP = 16
Q_SCALE = math.log2(math.e) * HEAD_DIM**-0.5
ROWS = (768, 384, 768, 384, 768, 1536)
STACKED = (False, True, False, True, False, True)


def dot(a, b):
    return jnp.dot(a, b, preferred_element_type=F32)


def layer_norm(values, gain):
    values = values.astype(F32)
    center = values - jnp.mean(values, axis=-1, keepdims=True)
    spread = jnp.mean(center * center, axis=-1, keepdims=True)
    return (center * lax.rsqrt(spread + 1e-05) * gain).astype(BF16)


def attend_pair(query, keys, vals):
    first = lax.broadcasted_iota(jnp.int32, (1, 128), 1) < HEAD_DIM
    zero = jnp.zeros_like(query)
    one = jnp.ones_like(vals)
    outs = []
    for mine in (first, jnp.logical_not(first)):
        scores = lax.dot_general(
            jnp.where(mine, query, zero), keys, (((1,), (1,)), ((), ())), preferred_element_type=F32
        )
        weights = jnp.exp2(scores).astype(BF16)
        filled = jnp.where(mine, vals, one)
        both = jnp.concatenate([filled * BF16(2.0**-8), filled * BF16(2.0**24)], axis=1)
        outs.append(dot(weights, both))
    out_a, out_b = outs
    low_top, low_sum = jnp.where(first, out_a[:, :128], out_b[:, :128]), jnp.where(
        first, out_b[:, :128], out_a[:, :128]
    )
    high_top, high_sum = jnp.where(first, out_a[:, 128:], out_b[:, 128:]), jnp.where(
        first, out_b[:, 128:], out_a[:, 128:]
    )
    low_sum = pltpu.roll(low_sum, HEAD_DIM, 1)
    high_sum = pltpu.roll(high_sum, HEAD_DIM, 1)
    large = low_sum > 2.0**-8
    return (jnp.where(large, low_top, high_top) / jnp.where(large, low_sum, high_sum)).astype(BF16)


def gelu(value):
    return 0.5 * value * (1.0 + lax.erf(value * 0.5**0.5))


def one_hot(rows_packed):
    packed = lax.broadcasted_iota(jnp.int32, (PACKED, PACKED), 0 if rows_packed else 1)
    plain = lax.broadcasted_iota(jnp.int32, (PACKED, PACKED), 1 if rows_packed else 0)
    device = (packed * 2731) >> 16
    rest = packed - device * 24
    return jnp.where(plain == ((rest >> 2) << 6) + ((rest & 3) << 4) + device, 1.0, 0.0).astype(BF16)


def pack(tokens, perm):
    sides = [
        jnp.concatenate([tokens[u * 64 : (u + 1) * 64, c * 128 : (c + 1) * 128] for c in range(6)], axis=0)
        for u in range(2)
    ]
    made = dot(perm, jnp.concatenate(sides, axis=1))
    return [made[:, u * 128 : (u + 1) * 128].reshape(16, 24, 128).astype(BF16) for u in range(2)]


def unpack(blocks, perm):
    sides = [blocks[u].astype(F32).reshape(PACKED, 128).astype(BF16) for u in range(2)]
    made = dot(perm, jnp.concatenate(sides, axis=1)).astype(BF16)
    return jnp.concatenate(
        [
            jnp.concatenate([made[c * 64 : (c + 1) * 64, u * 128 : (u + 1) * 128] for c in range(6)], axis=1)
            for u in range(2)
        ],
        axis=0,
    )


def kernel(
    clip, gain_s, gain_t, gain_m, w0, w1, w2, w3, w4, w5, out,
    x, normed, qkv_s, qkv_t, mixed, positions,
    send1, recv1, send2, recv2, cross1, cross2, perm,
    f0, f1, f2, f3, f4, f5,
    x_sem, own_sem, z_send, z_recv, ring_send, ring_recv, far_recv, core_send, core_recv, round_sem,
    a_send, a_recv, b_send, b_recv, c_send, c_recv, d_send, d_recv,
):
    s, m = lax.axis_index("seq"), lax.axis_index("mp")
    me = s * 2 + m
    z_hi, core = s // 32, lax.rem(s, 2)
    x_at, y_at = lax.rem(s // 8, 4), lax.rem(s // 2, 4)
    chip = lax.rem(x_at + y_at + z_hi * 2 + m, 4) * GROUP + x_at * 4 + y_at
    group, place = chip // GROUP, lax.rem(chip, GROUP)
    ring_place = x_at * (1 - core) + y_at * core
    above = (lax.rem(z_hi + m, 2) * 32 + lax.rem(s, 32), 1 - m)
    below = (lax.rem(z_hi + 1 - m, 2) * 32 + lax.rem(s, 32), 1 - m)
    owned = (w0, w1, w2, w3, w4, w5)
    full = (f0, f1, f2, f3, f4, f5)

    def part(k, half, start, rows):
        if STACKED[k]:
            return full[k].at[pl.ds(pl.multiple_of(half * ROWS[k] + start, 16), rows)]
        return full[k].at[half, pl.ds(pl.multiple_of(start, 16), rows)]

    def flip(bit):
        return me + bit * (1 - 2 * lax.rem(me // bit, 2))

    def device(index):
        return (index // 2, lax.rem(index, 2))

    def copy(ref, send_sem, recv_sem, to):
        pltpu.make_async_remote_copy(
            src_ref=ref, dst_ref=ref, send_sem=send_sem, recv_sem=recv_sem, device_id=to, device_id_type=MESH
        ).start()

    def landed(ref, sem):
        pltpu.make_async_copy(ref, ref, sem).wait()

    def load(k):
        if k in (0, 2):
            for c in range(3):
                columns = full[k].at[m, :, c * HALF : (c + 1) * HALF]
                pltpu.make_async_copy(owned[k].at[c], columns, own_sem.at[k]).start()
        else:
            pltpu.make_async_copy(owned[k], part(k, m, 0, ROWS[k]), own_sem.at[k]).start()

    def loaded(k):
        landed(part(k, m, 0, ROWS[k]), own_sem.at[k])

    def quarter(k, half, step, sub=None):
        rows = ROWS[k] // 8
        start = core * (ROWS[k] // 2) + lax.rem(ring_place + step + 4, 4) * rows
        if sub is None:
            return part(k, half, start, rows)
        if STACKED[k]:
            return part(k, half, start, rows).at[:, sub * HALF : (sub + 1) * HALF]
        return part(k, half, start + sub * (rows // 2), rows // 2)

    def ring(step):
        to_x, to_y = lax.rem(x_at + step * (1 - core) + 4, 4), lax.rem(y_at + step * core + 4, 4)
        return (z_hi * 32 + to_x * 8 + to_y * 2 + core, m)

    def fetch_z(k):
        loaded(k)
        for sub in range(2):
            copy(quarter(k, m, 0, sub), z_send.at[k], z_recv.at[k, sub], above if sub == 0 else below)

    def fetch_ring(k):
        for sub in range(2):
            landed(quarter(k, 1 - m, 0, sub), z_recv.at[k, sub])
        for way, step in enumerate((1, -1)):
            copy(quarter(k, 1 - m, 0), ring_send.at[k], ring_recv.at[k, way], ring(step))
        copy(quarter(k, 1 - m, 0), core_send.at[k], core_recv.at[k], device(flip(2)))

    def fetch_far(k):
        for way, step in enumerate((1, -1)):
            landed(quarter(k, 1 - m, -step), ring_recv.at[k, way])
            copy(quarter(k, 1 - m, -step, way), ring_send.at[k], far_recv.at[k, way], ring(step))
            copy(quarter(k, 1 - m, -step), core_send.at[k], core_recv.at[k], device(flip(2)))

    def fetch_last(k):
        for way in range(2):
            landed(quarter(k, 1 - m, 2, way), far_recv.at[k, way])
        copy(quarter(k, 1 - m, 2), core_send.at[k], core_recv.at[k], device(flip(2)))

    def fetched(k):
        landed(part(k, 0, 0, ROWS[k] // 2), core_recv.at[k])

    def exchange(p, b, to, send, recv, send_sem, recv_sem):
        def step(i):
            column = lax.rem(i + place, GROUP)
            dest = to * GROUP + column
            x_to, y_to = column // 4, lax.rem(column, 4)
            z_to = lax.rem(to + 8 - x_to - y_to, 4)
            pltpu.make_async_remote_copy(
                src_ref=send.at[p, dest],
                dst_ref=recv.at[p, chip],
                send_sem=send_sem.at[p],
                recv_sem=recv_sem.at[p, group],
                device_id=((z_to // 2) * 32 + x_to * 8 + y_to * 2 + core, lax.rem(z_to, 2)),
                device_id_type=MESH,
            ).start()

        @pl.when(b == 0)
        def _():
            pltpu.make_async_copy(send.at[p, chip], recv.at[p, chip], recv_sem.at[p, group]).start()

        @pl.when(b != 0)
        def _():
            step(0)

        for i in range(1, GROUP):
            step(i)

    def put(p, b, to, tokens, order, send, recv, send_sem, recv_sem):
        for block, to_core in zip(pack(tokens, perm[0]), order):
            send[p, pl.ds(to * GROUP, GROUP), to_core] = block
        exchange(p, b, to, send, recv, send_sem, recv_sem)

    def hand_on(p, source, recv, recv_sem, crossed, cross_send, cross_recv):
        chips = pl.ds(source * GROUP, GROUP)
        landed(recv.at[p, chips], recv_sem.at[p, source])
        pltpu.make_async_remote_copy(
            src_ref=recv.at[p, chips, 1 - core],
            dst_ref=crossed.at[p, chips],
            send_sem=cross_send.at[p],
            recv_sem=cross_recv.at[p, source],
            device_id=device(flip(2)),
            device_id_type=MESH,
        ).start()

    def take(p, source, recv, crossed, cross_recv):
        chips = pl.ds(source * GROUP, GROUP)
        landed(crossed.at[p, chips], cross_recv.at[p, source])
        return unpack((recv[p, chips, core], crossed[p, chips]), perm[1])

    barrier = pltpu.get_barrier_semaphore()
    greeted = [device(flip(bit)) for bit in (2, 8, 32, 64)] + [above, below]
    for step in (1, 3):
        greeted.append((z_hi * 32 + lax.rem(x_at + step, 4) * 8 + y_at * 2 + core, m))
        greeted.append((z_hi * 32 + x_at * 8 + lax.rem(y_at + step, 4) * 2 + core, m))
    for other in greeted:
        pl.semaphore_signal(barrier, inc=1, device_id=other, device_id_type=MESH)
    own_frames = pltpu.make_async_copy(clip.at[pl.ds(m * 4, 4)], x, x_sem)
    own_frames.start()
    for k in range(6):
        load(k)
    pl.semaphore_wait(barrier, len(greeted))
    fetch_z(0)
    fetch_z(1)
    perm[0] = one_hot(True)
    perm[1] = one_hot(False)
    own_frames.wait()

    @pl.loop(0, 4)
    def _(f):
        normed[pl.ds(pl.multiple_of(f * TOKENS, TOKENS), TOKENS)] = layer_norm(x[f], gain_s[...].reshape(1, D))

    columns = lax.broadcasted_iota(jnp.int32, (1, 3 * HALF), 1)
    scale = jnp.where(columns < HALF, Q_SCALE, 1.0).astype(F32)

    def spatial_qkv(half):
        @pl.loop(0, 4)
        def _(f):
            rows = pl.ds(pl.multiple_of(f * TOKENS, TOKENS), TOKENS)
            qkv_s[rows] = (dot(normed[rows], f0[half]) * scale).astype(BF16)

    def spatial_heads(half, f, start, count):
        rows = pl.ds(pl.multiple_of(f * TOKENS + start, count), count)
        every = pl.ds(pl.multiple_of(f * TOKENS, TOKENS), TOKENS)
        for pair in range(3):
            c = pair * 128
            mixed[rows, pl.ds(pl.multiple_of(half * HALF + c, 128), 128)] = attend_pair(
                qkv_s[rows, c : c + 128],
                qkv_s[every, HALF + c : HALF + c + 128],
                qkv_s[every, 2 * HALF + c : 2 * HALF + c + 128],
            )

    def rounds(low, high):
        for r in range(low, high):
            pl.semaphore_signal(
                round_sem.at[r], inc=1, device_id=device(flip((16, 32, 4, 8, 2, 1, 64)[r])), device_id_type=MESH
            )
            pl.semaphore_wait(round_sem.at[r], 1)

    spatial_qkv(m)
    fetch_ring(0)
    fetch_ring(1)
    fetch_z(2)
    fetch_z(3)
    rounds(0, 2)

    @pl.loop(0, 4)
    def _(f):
        @pl.when(f == 2)
        def _():
            fetch_far(0)
            fetch_far(1)
            fetch_z(4)
            fetch_z(5)
            rounds(2, 4)

        spatial_heads(m, f, 0, TOKENS)

    fetch_last(0)
    fetch_last(1)
    fetch_ring(2)
    fetch_ring(3)
    rounds(4, 7)
    fetched(0)
    spatial_qkv(1 - m)

    @pl.loop(0, 2)
    def _(p):
        @pl.when(p == 1)
        def _():
            fetch_last(2)
            fetch_last(3)
            fetch_ring(4)
            fetch_ring(5)

        @pl.loop(0, 4)
        def _(f):
            @pl.when(jnp.logical_and(p == 0, f == 2))
            def _():
                fetch_far(2)
                fetch_far(3)

            spatial_heads(1 - m, f, p * 128, 128)

        @pl.when(p == 0)
        def _():
            fetched(1)

        patches = pl.ds(pl.multiple_of(p * 128, 128), 128)

        @pl.loop(0, 2)
        def _(pair):
            rows = [pl.ds(pl.multiple_of((pair * 2 + i) * TOKENS + p * 128, 128), 128) for i in range(2)]
            total = dot(jnp.concatenate([mixed[r] for r in rows], axis=0), f1[...])
            for i in range(2):
                f = pair * 2 + i
                x[f, patches] = (x[f, patches].astype(F32) + total[i * 128 : (i + 1) * 128]).astype(BF16)

        @pl.loop(0, 4)
        def _(b):
            to = lax.rem(group + b, 4)
            tokens = [
                x[f, pl.ds(pl.multiple_of(p * 128 + u * CHIPS + to * GROUP, GROUP), GROUP)]
                for u in range(2)
                for f in range(4)
            ]
            put(p, b, to, jnp.concatenate(tokens, axis=0), (0, 1), send1, recv1, a_send, a_recv)

    fetched(2)

    def hand_on_a(p):
        @pl.loop(0, 4)
        def _(b):
            hand_on(p, lax.rem(group + 4 - b, 4), recv1, a_recv, cross1, c_send, c_recv)

    def hand_on_b(p):
        @pl.loop(0, 4)
        def _(b):
            hand_on(p, lax.rem(group + b, 4), recv2, b_recv, cross2, d_send, d_recv)

    hand_on_a(0)

    @pl.loop(0, 2)
    def _(p):
        @pl.loop(0, 2)
        def _(pair):
            rows = pl.ds(pl.multiple_of(p * 512 + pair * TOKENS, TOKENS), TOKENS)
            tokens = jnp.concatenate(
                [take(p, lax.rem(group + 4 - pair * 2 - i, 4), recv1, cross1, c_recv) for i in range(2)], axis=0
            )
            positions[rows] = tokens
            normal = layer_norm(tokens, gain_t[...].reshape(1, D))
            for half in range(2):
                qkv_t[half, rows] = (dot(normal, f2[half]) * scale).astype(BF16)

        @pl.when(p == 0)
        def _():
            fetch_far(4)
            fetch_far(5)

        @pl.loop(0, 4)
        def _(t):
            @pl.when(jnp.logical_and(p == 0, t == 2))
            def _():
                fetch_last(4)
                fetch_last(5)

            half = t // 2
            every = pl.ds(pl.multiple_of(p * 512, 512), 512)
            rows = pl.ds(pl.multiple_of(p * 512 + lax.rem(t, 2) * TOKENS, TOKENS), TOKENS)
            for pair in range(3):
                c = pair * 128
                mixed[rows, pl.ds(pl.multiple_of(half * HALF + c, 128), 128)] = attend_pair(
                    qkv_t[half, rows, c : c + 128],
                    qkv_t[half, every, HALF + c : HALF + c + 128],
                    qkv_t[half, every, 2 * HALF + c : 2 * HALF + c + 128],
                )

        @pl.when(p == 0)
        def _():
            fetched(3)
            fetched(4)
            fetched(5)
            hand_on_a(1)

        @pl.when(p == 1)
        def _():
            hand_on_b(0)

        @pl.loop(0, 2)
        def _(pair):
            rows = pl.ds(pl.multiple_of(p * 512 + pair * TOKENS, TOKENS), TOKENS)
            tokens = (positions[rows].astype(F32) + dot(mixed[rows], f3[...])).astype(BF16)
            normal = layer_norm(tokens, gain_m[...].reshape(1, D))
            total = tokens.astype(F32)
            for j in range(4):
                up = dot(normal, f4[j // 2, :, (j % 2) * D : (j % 2 + 1) * D])
                total = total + dot(gelu(up).astype(BF16), f5[j * D : (j + 1) * D])
            done = total.astype(BF16)
            for i in range(2):
                b = pair * 2 + i
                to = lax.rem(group + 4 - b, 4)
                put(p, b, to, done[i * 128 : (i + 1) * 128], (core, 1 - core), send2, recv2, b_send, b_recv)

    hand_on_b(1)

    @pl.loop(0, 2)
    def _(p):
        @pl.loop(0, 4)
        def _(b):
            source = lax.rem(group + b, 4)
            tokens = take(p, source, recv2, cross2, d_recv)
            for u, of_core in enumerate((core, 1 - core)):
                rows = pl.ds(pl.multiple_of(p * 128 + of_core * CHIPS + source * GROUP, GROUP), GROUP)
                for f in range(4):
                    out[f, rows] = tokens[u * 64 + f * 16 : u * 64 + (f + 1) * 16]

    for p in range(2):
        for send, sem in ((send1, a_send), (send2, b_send)):
            landed(send.at[p, pl.ds(0, CHIPS - 1)], sem.at[p])
        for crossed, sem in ((cross1, c_send), (cross2, d_send)):
            landed(crossed.at[p], sem.at[p])
    for k in range(6):
        landed(part(k, 0, 0, ROWS[k] // 8), z_send.at[k])
        landed(part(k, 0, 0, ROWS[k] // 8 * 3), ring_send.at[k])
        landed(part(k, 0, 0, ROWS[k] // 2), core_send.at[k])


def per_device(clip, gain_s, gain_t, gain_m, w0, w1, w2, w3, w4, w5):
    w0, w2 = jnp.swapaxes(w0, 0, 1), jnp.swapaxes(w2, 0, 1)
    vmem, anywhere = pl.BlockSpec(memory_space=pltpu.VMEM), pl.BlockSpec(memory_space=pl.ANY)
    dma = pltpu.SemaphoreType.DMA
    return pl.pallas_call(
        kernel,
        out_shape=jax.ShapeDtypeStruct((4, 256, D), BF16),
        in_specs=[anywhere, vmem, vmem, vmem] + [anywhere] * 6,
        out_specs=vmem,
        scratch_shapes=[
            pltpu.VMEM((4, 256, D), BF16),
            pltpu.VMEM((1024, D), BF16),
            pltpu.VMEM((1024, 3 * HALF), BF16),
            pltpu.VMEM((2, 1024, 3 * HALF), BF16),
            pltpu.VMEM((1024, D), BF16),
            pltpu.VMEM((1024, D), BF16),
            pltpu.VMEM((2, CHIPS, 2, 24, 128), BF16),
            pltpu.VMEM((2, CHIPS, 2, 24, 128), BF16),
            pltpu.VMEM((2, CHIPS, 2, 24, 128), BF16),
            pltpu.VMEM((2, CHIPS, 2, 24, 128), BF16),
            pltpu.VMEM((2, CHIPS, 24, 128), BF16),
            pltpu.VMEM((2, CHIPS, 24, 128), BF16),
            pltpu.VMEM((2, PACKED, PACKED), BF16),
            pltpu.VMEM((2, D, 3 * HALF), BF16),
            pltpu.VMEM((D, D), BF16),
            pltpu.VMEM((2, D, 3 * HALF), BF16),
            pltpu.VMEM((D, D), BF16),
            pltpu.VMEM((2, D, 1536), BF16),
            pltpu.VMEM((3072, D), BF16),
            dma,
            dma((6,)),
            dma((6,)),
            dma((6, 2)),
            dma((6,)),
            dma((6, 2)),
            dma((6, 2)),
            dma((6,)),
            dma((6,)),
            pltpu.SemaphoreType.REGULAR((7,)),
            dma((2,)),
            dma((2, 4)),
            dma((2,)),
            dma((2, 4)),
            dma((2,)),
            dma((2, 4)),
            dma((2,)),
            dma((2, 4)),
        ],
        compiler_params=pltpu.CompilerParams(
            collective_id=0, has_side_effects=True, vmem_limit_bytes=60 << 20
        ),
        cost_estimate=pl.CostEstimate(
            flops=22 * 10**9, bytes_accessed=13 * 10**6, transcendentals=12 * 10**6
        ),
    )(clip, gain_s, gain_t, gain_m, w0, w1, w2, w3, w4, w5)


def solution(mesh):
    return jax.shard_map(
        per_device,
        mesh=mesh,
        in_specs=(
            P("seq", None, None),
            P(),
            P(),
            P(),
            P(None, None, "mp"),
            P("mp", None),
            P(None, None, "mp"),
            P("mp", None),
            P(None, "mp"),
            P("mp", None),
        ),
        out_specs=P(("seq", "mp"), None, None),
        check_vma=False,
    )
```

```python
import functools
import math

import jax
import jax.numpy as jnp
from jax import lax
from jax.experimental import pallas as pl
from jax.experimental.pallas import tpu as pltpu
from jax.sharding import PartitionSpec as P

MESH = pl.DeviceIdType.MESH
F32, BF16 = jnp.float32, jnp.bfloat16
HEAD_DIM = 64
D = 768
HALF = 384
TOKENS = 256
CHIPS = 64
PACKED = 16 * 24
GROUP = 16
Q_SCALE = math.log2(math.e) * HEAD_DIM**-0.5
ROWS = (768, 384, 768, 384, 768, 1536)
STACKED = (False, True, False, True, False, True)


def dot(a, b):
    return jnp.dot(a, b, preferred_element_type=F32)


def layer_norm(values, gain):
    values = values.astype(F32)
    center = values - jnp.mean(values, axis=-1, keepdims=True)
    spread = jnp.mean(center * center, axis=-1, keepdims=True)
    return (center * lax.rsqrt(spread + 1e-05) * gain).astype(BF16)


def attend_pair(query, keys, vals):
    first = lax.broadcasted_iota(jnp.int32, (1, 128), 1) < HEAD_DIM
    zero = jnp.zeros_like(query)
    one = jnp.ones_like(vals)
    outs = []
    for mine in (first, jnp.logical_not(first)):
        scores = lax.dot_general(
            jnp.where(mine, query, zero), keys, (((1,), (1,)), ((), ())), preferred_element_type=F32
        )
        weights = jnp.exp2(scores).astype(BF16)
        filled = jnp.where(mine, vals, one)
        both = jnp.concatenate([filled * BF16(2.0**-8), filled * BF16(2.0**24)], axis=1)
        outs.append(dot(weights, both))
    out_a, out_b = outs
    low_top, low_sum = jnp.where(first, out_a[:, :128], out_b[:, :128]), jnp.where(
        first, out_b[:, :128], out_a[:, :128]
    )
    high_top, high_sum = jnp.where(first, out_a[:, 128:], out_b[:, 128:]), jnp.where(
        first, out_b[:, 128:], out_a[:, 128:]
    )
    low_sum = pltpu.roll(low_sum, HEAD_DIM, 1)
    high_sum = pltpu.roll(high_sum, HEAD_DIM, 1)
    large = low_sum > 2.0**-8
    return (jnp.where(large, low_top, high_top) / jnp.where(large, low_sum, high_sum)).astype(BF16)


def gelu(value):
    return 0.5 * value * (1.0 + lax.erf(value * 0.5**0.5))


def one_hot(rows_packed):
    packed = lax.broadcasted_iota(jnp.int32, (PACKED, PACKED), 0 if rows_packed else 1)
    plain = lax.broadcasted_iota(jnp.int32, (PACKED, PACKED), 1 if rows_packed else 0)
    device = (packed * 2731) >> 16
    rest = packed - device * 24
    return jnp.where(plain == ((rest >> 2) << 6) + ((rest & 3) << 4) + device, 1.0, 0.0).astype(BF16)


def pack(tokens, perm):
    sides = [
        jnp.concatenate([tokens[u * 64 : (u + 1) * 64, c * 128 : (c + 1) * 128] for c in range(6)], axis=0)
        for u in range(2)
    ]
    made = dot(perm, jnp.concatenate(sides, axis=1))
    return [made[:, u * 128 : (u + 1) * 128].reshape(16, 24, 128).astype(BF16) for u in range(2)]


def unpack(blocks, perm):
    sides = [blocks[u].astype(F32).reshape(PACKED, 128).astype(BF16) for u in range(2)]
    made = dot(perm, jnp.concatenate(sides, axis=1)).astype(BF16)
    return jnp.concatenate(
        [
            jnp.concatenate([made[c * 64 : (c + 1) * 64, u * 128 : (u + 1) * 128] for c in range(6)], axis=1)
            for u in range(2)
        ],
        axis=0,
    )


def kernel(
    clip, gain_s, gain_t, gain_m, w0, w1, w2, w3, w4, w5, out,
    x, normed, qkv_s, qkv_t, mixed, positions,
    send1, recv1, send2, recv2, cross1, cross2, perm,
    f0, f1, f2, f3, f4, f5,
    x_sem, own_sem, z_send, z_recv, ring_send, ring_recv, far_recv, core_send, core_recv, round_sem,
    a_send, a_recv, b_send, b_recv, c_send, c_recv, d_send, d_recv,
):
    s, m = lax.axis_index("seq"), lax.axis_index("mp")
    me = s * 2 + m
    z_hi, core = s // 32, lax.rem(s, 2)
    x_at, y_at = lax.rem(s // 8, 4), lax.rem(s // 2, 4)
    chip = lax.rem(x_at + y_at + z_hi * 2 + m, 4) * GROUP + x_at * 4 + y_at
    group, place = chip // GROUP, lax.rem(chip, GROUP)
    ring_place = x_at * (1 - core) + y_at * core
    above = (lax.rem(z_hi + m, 2) * 32 + lax.rem(s, 32), 1 - m)
    below = (lax.rem(z_hi + 1 - m, 2) * 32 + lax.rem(s, 32), 1 - m)
    owned = (w0, w1, w2, w3, w4, w5)
    full = (f0, f1, f2, f3, f4, f5)

    def part(k, half, start, rows):
        if STACKED[k]:
            return full[k].at[pl.ds(pl.multiple_of(half * ROWS[k] + start, 16), rows)]
        return full[k].at[half, pl.ds(pl.multiple_of(start, 16), rows)]

    def flip(bit):
        return me + bit * (1 - 2 * lax.rem(me // bit, 2))

    def device(index):
        return (index // 2, lax.rem(index, 2))

    def copy(ref, send_sem, recv_sem, to):
        pltpu.make_async_remote_copy(
            src_ref=ref, dst_ref=ref, send_sem=send_sem, recv_sem=recv_sem, device_id=to, device_id_type=MESH
        ).start()

    def landed(ref, sem):
        pltpu.make_async_copy(ref, ref, sem).wait()

    def load(k):
        if k in (0, 2):
            for c in range(3):
                columns = full[k].at[m, :, c * HALF : (c + 1) * HALF]
                pltpu.make_async_copy(owned[k].at[c], columns, own_sem.at[k]).start()
        else:
            pltpu.make_async_copy(owned[k], part(k, m, 0, ROWS[k]), own_sem.at[k]).start()

    def loaded(k):
        landed(part(k, m, 0, ROWS[k]), own_sem.at[k])

    def quarter(k, half, step, sub=None):
        rows = ROWS[k] // 8
        start = core * (ROWS[k] // 2) + lax.rem(ring_place + step + 4, 4) * rows
        if sub is None:
            return part(k, half, start, rows)
        if STACKED[k]:
            return part(k, half, start, rows).at[:, sub * HALF : (sub + 1) * HALF]
        return part(k, half, start + sub * (rows // 2), rows // 2)

    def ring(step):
        to_x, to_y = lax.rem(x_at + step * (1 - core) + 4, 4), lax.rem(y_at + step * core + 4, 4)
        return (z_hi * 32 + to_x * 8 + to_y * 2 + core, m)

    def fetch_z(k):
        loaded(k)
        for sub in range(2):
            copy(quarter(k, m, 0, sub), z_send.at[k], z_recv.at[k, sub], above if sub == 0 else below)

    def fetch_ring(k):
        for sub in range(2):
            landed(quarter(k, 1 - m, 0, sub), z_recv.at[k, sub])
        for way, step in enumerate((1, -1)):
            copy(quarter(k, 1 - m, 0), ring_send.at[k], ring_recv.at[k, way], ring(step))
        copy(quarter(k, 1 - m, 0), core_send.at[k], core_recv.at[k], device(flip(2)))

    def fetch_far(k):
        for way, step in enumerate((1, -1)):
            landed(quarter(k, 1 - m, -step), ring_recv.at[k, way])
            copy(quarter(k, 1 - m, -step, way), ring_send.at[k], far_recv.at[k, way], ring(step))
            copy(quarter(k, 1 - m, -step), core_send.at[k], core_recv.at[k], device(flip(2)))

    def fetch_last(k):
        for way in range(2):
            landed(quarter(k, 1 - m, 2, way), far_recv.at[k, way])
        copy(quarter(k, 1 - m, 2), core_send.at[k], core_recv.at[k], device(flip(2)))

    def fetched(k):
        landed(part(k, 0, 0, ROWS[k] // 2), core_recv.at[k])

    def exchange(p, b, to, send, recv, send_sem, recv_sem):
        def step(i):
            column = lax.rem(i + place, GROUP)
            dest = to * GROUP + column
            x_to, y_to = column // 4, lax.rem(column, 4)
            z_to = lax.rem(to + 8 - x_to - y_to, 4)
            pltpu.make_async_remote_copy(
                src_ref=send.at[p, dest],
                dst_ref=recv.at[p, chip],
                send_sem=send_sem.at[p],
                recv_sem=recv_sem.at[p, group],
                device_id=((z_to // 2) * 32 + x_to * 8 + y_to * 2 + core, lax.rem(z_to, 2)),
                device_id_type=MESH,
            ).start()

        @pl.when(b == 0)
        def _():
            pltpu.make_async_copy(send.at[p, chip], recv.at[p, chip], recv_sem.at[p, group]).start()

        @pl.when(b != 0)
        def _():
            step(0)

        for i in range(1, GROUP):
            step(i)

    def put(p, b, to, tokens, order, send, recv, send_sem, recv_sem):
        for block, to_core in zip(pack(tokens, perm[0]), order):
            send[p, pl.ds(to * GROUP, GROUP), to_core] = block
        exchange(p, b, to, send, recv, send_sem, recv_sem)

    def hand_on(p, source, recv, recv_sem, crossed, cross_send, cross_recv):
        chips = pl.ds(source * GROUP, GROUP)
        landed(recv.at[p, chips], recv_sem.at[p, source])
        pltpu.make_async_remote_copy(
            src_ref=recv.at[p, chips, 1 - core],
            dst_ref=crossed.at[p, chips],
            send_sem=cross_send.at[p],
            recv_sem=cross_recv.at[p, source],
            device_id=device(flip(2)),
            device_id_type=MESH,
        ).start()

    def take(p, source, recv, crossed, cross_recv):
        chips = pl.ds(source * GROUP, GROUP)
        landed(crossed.at[p, chips], cross_recv.at[p, source])
        return unpack((recv[p, chips, core], crossed[p, chips]), perm[1])

    def greet(r):
        if r > 0:
            pl.semaphore_wait(round_sem.at[r - 1], 1)
        if r < 7:
            pl.semaphore_signal(
                round_sem.at[r], inc=1, device_id=device(flip((16, 32, 4, 8, 2, 1, 64)[r])), device_id_type=MESH
            )

    barrier = pltpu.get_barrier_semaphore()
    greeted = [device(flip(bit)) for bit in (2, 8, 32, 64)] + [above, below]
    for step in (1, 3):
        greeted.append((z_hi * 32 + lax.rem(x_at + step, 4) * 8 + y_at * 2 + core, m))
        greeted.append((z_hi * 32 + x_at * 8 + lax.rem(y_at + step, 4) * 2 + core, m))
    for other in greeted:
        pl.semaphore_signal(barrier, inc=1, device_id=other, device_id_type=MESH)
    own_frames = pltpu.make_async_copy(clip.at[pl.ds(m * 4, 4)], x, x_sem)
    own_frames.start()
    for k in range(6):
        load(k)
    pl.semaphore_wait(barrier, len(greeted))
    fetch_z(0)
    fetch_z(1)
    greet(0)
    perm[0] = one_hot(True)
    perm[1] = one_hot(False)
    own_frames.wait()

    @pl.loop(0, 4)
    def _(f):
        normed[pl.ds(pl.multiple_of(f * TOKENS, TOKENS), TOKENS)] = layer_norm(x[f], gain_s[...].reshape(1, D))

    columns = lax.broadcasted_iota(jnp.int32, (1, 3 * HALF), 1)
    scale = jnp.where(columns < HALF, Q_SCALE, 1.0).astype(F32)

    def spatial_qkv(half):
        @pl.loop(0, 4)
        def _(f):
            rows = pl.ds(pl.multiple_of(f * TOKENS, TOKENS), TOKENS)
            qkv_s[rows] = (dot(normed[rows], f0[half]) * scale).astype(BF16)

    def spatial_heads(half, f, start, count):
        rows = pl.ds(pl.multiple_of(f * TOKENS + start, count), count)
        every = pl.ds(pl.multiple_of(f * TOKENS, TOKENS), TOKENS)
        for pair in range(3):
            c = pair * 128
            mixed[rows, pl.ds(pl.multiple_of(half * HALF + c, 128), 128)] = attend_pair(
                qkv_s[rows, c : c + 128],
                qkv_s[every, HALF + c : HALF + c + 128],
                qkv_s[every, 2 * HALF + c : 2 * HALF + c + 128],
            )

    greet(1)
    spatial_qkv(m)
    fetch_ring(0)
    fetch_ring(1)
    fetch_z(2)
    fetch_z(3)
    greet(2)

    @pl.loop(0, 4)
    def _(f):
        @pl.when(f == 2)
        def _():
            fetch_far(0)
            fetch_far(1)
            fetch_z(4)
            fetch_z(5)
            greet(4)

        @pl.when(f == 1)
        def _():
            greet(3)

        @pl.when(f == 3)
        def _():
            greet(5)

        spatial_heads(m, f, 0, TOKENS)

    fetch_last(0)
    fetch_last(1)
    fetch_ring(2)
    fetch_ring(3)
    greet(6)
    fetched(0)
    spatial_qkv(1 - m)
    greet(7)

    @pl.loop(0, 2)
    def _(p):
        @pl.when(p == 1)
        def _():
            fetch_last(2)
            fetch_last(3)
            fetch_ring(4)
            fetch_ring(5)

        @pl.loop(0, 4)
        def _(f):
            @pl.when(jnp.logical_and(p == 0, f == 2))
            def _():
                fetch_far(2)
                fetch_far(3)

            spatial_heads(1 - m, f, p * 128, 128)

        @pl.when(p == 0)
        def _():
            fetched(1)

        patches = pl.ds(pl.multiple_of(p * 128, 128), 128)

        @pl.loop(0, 2)
        def _(pair):
            rows = [pl.ds(pl.multiple_of((pair * 2 + i) * TOKENS + p * 128, 128), 128) for i in range(2)]
            total = dot(jnp.concatenate([mixed[r] for r in rows], axis=0), f1[...])
            for i in range(2):
                f = pair * 2 + i
                x[f, patches] = (x[f, patches].astype(F32) + total[i * 128 : (i + 1) * 128]).astype(BF16)

        @pl.loop(0, 4)
        def _(b):
            to = lax.rem(group + b, 4)
            tokens = [
                x[f, pl.ds(pl.multiple_of(p * 128 + u * CHIPS + to * GROUP, GROUP), GROUP)]
                for u in range(2)
                for f in range(4)
            ]
            put(p, b, to, jnp.concatenate(tokens, axis=0), (0, 1), send1, recv1, a_send, a_recv)

    fetched(2)

    def hand_on_a(p):
        @pl.loop(0, 4)
        def _(b):
            hand_on(p, lax.rem(group + 4 - b, 4), recv1, a_recv, cross1, c_send, c_recv)

    def hand_on_b(p):
        @pl.loop(0, 4)
        def _(b):
            hand_on(p, lax.rem(group + b, 4), recv2, b_recv, cross2, d_send, d_recv)

    hand_on_a(0)

    @pl.loop(0, 2)
    def _(p):
        @pl.loop(0, 2)
        def _(pair):
            rows = pl.ds(pl.multiple_of(p * 512 + pair * TOKENS, TOKENS), TOKENS)
            tokens = jnp.concatenate(
                [take(p, lax.rem(group + 4 - pair * 2 - i, 4), recv1, cross1, c_recv) for i in range(2)], axis=0
            )
            positions[rows] = tokens
            normal = layer_norm(tokens, gain_t[...].reshape(1, D))
            for half in range(2):
                qkv_t[half, rows] = (dot(normal, f2[half]) * scale).astype(BF16)

        @pl.loop(0, 4)
        def _(t):
            @pl.when(jnp.logical_and(p == 0, t == 1))
            def _():
                fetch_far(4)
                fetch_far(5)

            @pl.when(jnp.logical_and(p == 0, t == 3))
            def _():
                fetch_last(4)
                fetch_last(5)

            half = t // 2
            every = pl.ds(pl.multiple_of(p * 512, 512), 512)
            rows = pl.ds(pl.multiple_of(p * 512 + lax.rem(t, 2) * TOKENS, TOKENS), TOKENS)
            for pair in range(3):
                c = pair * 128
                mixed[rows, pl.ds(pl.multiple_of(half * HALF + c, 128), 128)] = attend_pair(
                    qkv_t[half, rows, c : c + 128],
                    qkv_t[half, every, HALF + c : HALF + c + 128],
                    qkv_t[half, every, 2 * HALF + c : 2 * HALF + c + 128],
                )

        @pl.when(p == 0)
        def _():
            fetched(3)
            fetched(4)
            fetched(5)
            hand_on_a(1)

        @pl.when(p == 1)
        def _():
            hand_on_b(0)

        @pl.loop(0, 2)
        def _(pair):
            rows = pl.ds(pl.multiple_of(p * 512 + pair * TOKENS, TOKENS), TOKENS)
            tokens = (positions[rows].astype(F32) + dot(mixed[rows], f3[...])).astype(BF16)
            normal = layer_norm(tokens, gain_m[...].reshape(1, D))
            total = tokens.astype(F32)
            for j in range(4):
                up = dot(normal, f4[j // 2, :, (j % 2) * D : (j % 2 + 1) * D])
                total = total + dot(gelu(up).astype(BF16), f5[j * D : (j + 1) * D])
            done = total.astype(BF16)
            for i in range(2):
                b = pair * 2 + i
                to = lax.rem(group + 4 - b, 4)
                put(p, b, to, done[i * 128 : (i + 1) * 128], (core, 1 - core), send2, recv2, b_send, b_recv)

    hand_on_b(1)

    @pl.loop(0, 2)
    def _(p):
        @pl.loop(0, 4)
        def _(b):
            source = lax.rem(group + b, 4)
            tokens = take(p, source, recv2, cross2, d_recv)
            for u, of_core in enumerate((core, 1 - core)):
                rows = pl.ds(pl.multiple_of(p * 128 + of_core * CHIPS + source * GROUP, GROUP), GROUP)
                for f in range(4):
                    out[f, rows] = tokens[u * 64 + f * 16 : u * 64 + (f + 1) * 16]

    for p in range(2):
        for send, sem in ((send1, a_send), (send2, b_send)):
            landed(send.at[p, pl.ds(0, CHIPS - 1)], sem.at[p])
        for crossed, sem in ((cross1, c_send), (cross2, d_send)):
            landed(crossed.at[p], sem.at[p])
    for k in range(6):
        landed(part(k, 0, 0, ROWS[k] // 8), z_send.at[k])
        landed(part(k, 0, 0, ROWS[k] // 8 * 3), ring_send.at[k])
        landed(part(k, 0, 0, ROWS[k] // 2), core_send.at[k])


def per_device(clip, gain_s, gain_t, gain_m, w0, w1, w2, w3, w4, w5):
    w0, w2 = jnp.swapaxes(w0, 0, 1), jnp.swapaxes(w2, 0, 1)
    vmem, anywhere = pl.BlockSpec(memory_space=pltpu.VMEM), pl.BlockSpec(memory_space=pl.ANY)
    dma = pltpu.SemaphoreType.DMA
    return pl.pallas_call(
        kernel,
        out_shape=jax.ShapeDtypeStruct((4, 256, D), BF16),
        in_specs=[anywhere, vmem, vmem, vmem] + [anywhere] * 6,
        out_specs=vmem,
        scratch_shapes=[
            pltpu.VMEM((4, 256, D), BF16),
            pltpu.VMEM((1024, D), BF16),
            pltpu.VMEM((1024, 3 * HALF), BF16),
            pltpu.VMEM((2, 1024, 3 * HALF), BF16),
            pltpu.VMEM((1024, D), BF16),
            pltpu.VMEM((1024, D), BF16),
            pltpu.VMEM((2, CHIPS, 2, 24, 128), BF16),
            pltpu.VMEM((2, CHIPS, 2, 24, 128), BF16),
            pltpu.VMEM((2, CHIPS, 2, 24, 128), BF16),
            pltpu.VMEM((2, CHIPS, 2, 24, 128), BF16),
            pltpu.VMEM((2, CHIPS, 24, 128), BF16),
            pltpu.VMEM((2, CHIPS, 24, 128), BF16),
            pltpu.VMEM((2, PACKED, PACKED), BF16),
            pltpu.VMEM((2, D, 3 * HALF), BF16),
            pltpu.VMEM((D, D), BF16),
            pltpu.VMEM((2, D, 3 * HALF), BF16),
            pltpu.VMEM((D, D), BF16),
            pltpu.VMEM((2, D, 1536), BF16),
            pltpu.VMEM((3072, D), BF16),
            dma,
            dma((6,)),
            dma((6,)),
            dma((6, 2)),
            dma((6,)),
            dma((6, 2)),
            dma((6, 2)),
            dma((6,)),
            dma((6,)),
            pltpu.SemaphoreType.REGULAR((7,)),
            dma((2,)),
            dma((2, 4)),
            dma((2,)),
            dma((2, 4)),
            dma((2,)),
            dma((2, 4)),
            dma((2,)),
            dma((2, 4)),
        ],
        compiler_params=pltpu.CompilerParams(
            collective_id=0, has_side_effects=True, vmem_limit_bytes=60 << 20
        ),
        cost_estimate=pl.CostEstimate(
            flops=22 * 10**9, bytes_accessed=13 * 10**6, transcendentals=12 * 10**6
        ),
    )(clip, gain_s, gain_t, gain_m, w0, w1, w2, w3, w4, w5)


def solution(mesh):
    return jax.shard_map(
        per_device,
        mesh=mesh,
        in_specs=(
            P("seq", None, None),
            P(),
            P(),
            P(),
            P(None, None, "mp"),
            P("mp", None),
            P(None, None, "mp"),
            P("mp", None),
            P(None, "mp"),
            P("mp", None),
        ),
        out_specs=P(("seq", "mp"), None, None),
        check_vma=False,
    )
```

```python
import functools
import math

import jax
import jax.numpy as jnp
from jax import lax
from jax.experimental import pallas as pl
from jax.experimental.pallas import tpu as pltpu
from jax.sharding import PartitionSpec as P

MESH = pl.DeviceIdType.MESH
F32, BF16 = jnp.float32, jnp.bfloat16
HEAD_DIM = 64
D = 768
HALF = 384
TOKENS = 256
CHIPS = 64
PACKED = 16 * 24
GROUP = 16
Q_SCALE = math.log2(math.e) * HEAD_DIM**-0.5
ROWS = (768, 384, 768, 384, 768, 1536)
STACKED = (False, True, False, True, False, True)


def dot(a, b):
    return jnp.dot(a, b, preferred_element_type=F32)


def layer_norm(values, gain):
    values = values.astype(F32)
    center = values - jnp.mean(values, axis=-1, keepdims=True)
    spread = jnp.mean(center * center, axis=-1, keepdims=True)
    return (center * lax.rsqrt(spread + 1e-05) * gain).astype(BF16)


def attend_pair(query, keys, vals):
    first = lax.broadcasted_iota(jnp.int32, (1, 128), 1) < HEAD_DIM
    zero = jnp.zeros_like(query)
    one = jnp.ones_like(vals)
    outs = []
    for mine in (first, jnp.logical_not(first)):
        scores = lax.dot_general(
            jnp.where(mine, query, zero), keys, (((1,), (1,)), ((), ())), preferred_element_type=F32
        )
        weights = jnp.exp2(scores).astype(BF16)
        filled = jnp.where(mine, vals, one)
        both = jnp.concatenate([filled * BF16(2.0**-8), filled * BF16(2.0**24)], axis=1)
        outs.append(dot(weights, both))
    out_a, out_b = outs
    low_top, low_sum = jnp.where(first, out_a[:, :128], out_b[:, :128]), jnp.where(
        first, out_b[:, :128], out_a[:, :128]
    )
    high_top, high_sum = jnp.where(first, out_a[:, 128:], out_b[:, 128:]), jnp.where(
        first, out_b[:, 128:], out_a[:, 128:]
    )
    low_sum = pltpu.roll(low_sum, HEAD_DIM, 1)
    high_sum = pltpu.roll(high_sum, HEAD_DIM, 1)
    large = low_sum > 2.0**-8
    return (jnp.where(large, low_top, high_top) / jnp.where(large, low_sum, high_sum)).astype(BF16)


def gelu(value):
    return 0.5 * value * (1.0 + lax.erf(value * 0.5**0.5))


def one_hot(rows_packed):
    packed = lax.broadcasted_iota(jnp.int32, (PACKED, PACKED), 0 if rows_packed else 1)
    plain = lax.broadcasted_iota(jnp.int32, (PACKED, PACKED), 1 if rows_packed else 0)
    device = (packed * 2731) >> 16
    rest = packed - device * 24
    return jnp.where(plain == ((rest >> 2) << 6) + ((rest & 3) << 4) + device, 1.0, 0.0).astype(BF16)


def pack(tokens, perm):
    sides = [
        jnp.concatenate([tokens[u * 64 : (u + 1) * 64, c * 128 : (c + 1) * 128] for c in range(6)], axis=0)
        for u in range(2)
    ]
    made = dot(perm, jnp.concatenate(sides, axis=1))
    return [made[:, u * 128 : (u + 1) * 128].reshape(16, 24, 128).astype(BF16) for u in range(2)]


def unpack(blocks, perm):
    sides = [blocks[u].astype(F32).reshape(PACKED, 128).astype(BF16) for u in range(2)]
    made = dot(perm, jnp.concatenate(sides, axis=1)).astype(BF16)
    return jnp.concatenate(
        [
            jnp.concatenate([made[c * 64 : (c + 1) * 64, u * 128 : (u + 1) * 128] for c in range(6)], axis=1)
            for u in range(2)
        ],
        axis=0,
    )


def kernel(
    clip, gain_s, gain_t, gain_m, w0, w1, w2, w3, w4, w5, out,
    x, normed, qkv_s, qkv_t, mixed, positions,
    send1, recv1, send2, recv2, cross1, cross2, perm,
    f0, f1, f2, f3, f4, f5,
    x_sem, own_sem, z_send, z_recv, ring_send, ring_recv, far_recv, core_send, core_recv, round_sem,
    a_send, a_recv, b_send, b_recv, c_send, c_recv, d_send, d_recv,
):
    s, m = lax.axis_index("seq"), lax.axis_index("mp")
    me = s * 2 + m
    z_hi, core = s // 32, lax.rem(s, 2)
    x_at, y_at = lax.rem(s // 8, 4), lax.rem(s // 2, 4)
    chip = lax.rem(x_at + y_at + z_hi * 2 + m, 4) * GROUP + x_at * 4 + y_at
    group, place = chip // GROUP, lax.rem(chip, GROUP)
    ring_place = x_at * (1 - core) + y_at * core
    above = (lax.rem(z_hi + m, 2) * 32 + lax.rem(s, 32), 1 - m)
    below = (lax.rem(z_hi + 1 - m, 2) * 32 + lax.rem(s, 32), 1 - m)
    owned = (w0, w1, w2, w3, w4, w5)
    full = (f0, f1, f2, f3, f4, f5)

    def part(k, half, start, rows):
        if STACKED[k]:
            return full[k].at[pl.ds(pl.multiple_of(half * ROWS[k] + start, 16), rows)]
        return full[k].at[half, pl.ds(pl.multiple_of(start, 16), rows)]

    def flip(bit):
        return me + bit * (1 - 2 * lax.rem(me // bit, 2))

    def device(index):
        return (index // 2, lax.rem(index, 2))

    def copy(ref, send_sem, recv_sem, to):
        pltpu.make_async_remote_copy(
            src_ref=ref, dst_ref=ref, send_sem=send_sem, recv_sem=recv_sem, device_id=to, device_id_type=MESH
        ).start()

    def landed(ref, sem):
        pltpu.make_async_copy(ref, ref, sem).wait()

    def load(k):
        if k in (0, 2):
            for c in range(3):
                columns = full[k].at[m, :, c * HALF : (c + 1) * HALF]
                pltpu.make_async_copy(owned[k].at[c], columns, own_sem.at[k]).start()
        else:
            pltpu.make_async_copy(owned[k], part(k, m, 0, ROWS[k]), own_sem.at[k]).start()

    def loaded(k):
        landed(part(k, m, 0, ROWS[k]), own_sem.at[k])

    def quarter(k, half, step, sub=None):
        rows = ROWS[k] // 8
        start = core * (ROWS[k] // 2) + lax.rem(ring_place + step + 4, 4) * rows
        if sub is None:
            return part(k, half, start, rows)
        if STACKED[k]:
            return part(k, half, start, rows).at[:, sub * HALF : (sub + 1) * HALF]
        return part(k, half, start + sub * (rows // 2), rows // 2)

    def ring(step):
        to_x, to_y = lax.rem(x_at + step * (1 - core) + 4, 4), lax.rem(y_at + step * core + 4, 4)
        return (z_hi * 32 + to_x * 8 + to_y * 2 + core, m)

    def fetch_z(k):
        loaded(k)
        for sub in range(2):
            copy(quarter(k, m, 0, sub), z_send.at[k], z_recv.at[k, sub], above if sub == 0 else below)

    def fetch_ring(k):
        for sub in range(2):
            landed(quarter(k, 1 - m, 0, sub), z_recv.at[k, sub])
        for way, step in enumerate((1, -1)):
            copy(quarter(k, 1 - m, 0), ring_send.at[k], ring_recv.at[k, way], ring(step))
        copy(quarter(k, 1 - m, 0), core_send.at[k], core_recv.at[k], device(flip(2)))

    def fetch_far(k):
        for way, step in enumerate((1, -1)):
            landed(quarter(k, 1 - m, -step), ring_recv.at[k, way])
            copy(quarter(k, 1 - m, -step, way), ring_send.at[k], far_recv.at[k, way], ring(step))
            copy(quarter(k, 1 - m, -step), core_send.at[k], core_recv.at[k], device(flip(2)))

    def fetch_last(k):
        for way in range(2):
            landed(quarter(k, 1 - m, 2, way), far_recv.at[k, way])
        copy(quarter(k, 1 - m, 2), core_send.at[k], core_recv.at[k], device(flip(2)))

    def fetched(k):
        landed(part(k, 0, 0, ROWS[k] // 2), core_recv.at[k])

    def exchange(p, b, to, send, recv, send_sem, recv_sem):
        def step(i):
            column = lax.rem(i + place, GROUP)
            dest = to * GROUP + column
            x_to, y_to = column // 4, lax.rem(column, 4)
            z_to = lax.rem(to + 8 - x_to - y_to, 4)
            pltpu.make_async_remote_copy(
                src_ref=send.at[p, dest],
                dst_ref=recv.at[p, chip],
                send_sem=send_sem.at[p],
                recv_sem=recv_sem.at[p, group],
                device_id=((z_to // 2) * 32 + x_to * 8 + y_to * 2 + core, lax.rem(z_to, 2)),
                device_id_type=MESH,
            ).start()

        @pl.when(b == 0)
        def _():
            pltpu.make_async_copy(send.at[p, chip], recv.at[p, chip], recv_sem.at[p, group]).start()

        @pl.when(b != 0)
        def _():
            step(0)

        for i in range(1, GROUP):
            step(i)

    def put(p, b, to, tokens, order, send, recv, send_sem, recv_sem):
        for block, to_core in zip(pack(tokens, perm[0]), order):
            send[p, pl.ds(to * GROUP, GROUP), to_core] = block
        exchange(p, b, to, send, recv, send_sem, recv_sem)

    def hand_on(p, source, recv, recv_sem, crossed, cross_send, cross_recv):
        chips = pl.ds(source * GROUP, GROUP)
        landed(recv.at[p, chips], recv_sem.at[p, source])
        pltpu.make_async_remote_copy(
            src_ref=recv.at[p, chips, 1 - core],
            dst_ref=crossed.at[p, chips],
            send_sem=cross_send.at[p],
            recv_sem=cross_recv.at[p, source],
            device_id=device(flip(2)),
            device_id_type=MESH,
        ).start()

    def take(p, source, recv, crossed, cross_recv):
        chips = pl.ds(source * GROUP, GROUP)
        landed(crossed.at[p, chips], cross_recv.at[p, source])
        return unpack((recv[p, chips, core], crossed[p, chips]), perm[1])

    def greet(r):
        if r > 0:
            pl.semaphore_wait(round_sem.at[r - 1], 1)
        if r < 7:
            pl.semaphore_signal(
                round_sem.at[r], inc=1, device_id=device(flip((16, 32, 4, 8, 2, 1, 64)[r])), device_id_type=MESH
            )

    barrier = pltpu.get_barrier_semaphore()
    greeted = [device(flip(bit)) for bit in (2, 8, 32, 64)] + [above, below]
    for step in (1, 3):
        greeted.append((z_hi * 32 + lax.rem(x_at + step, 4) * 8 + y_at * 2 + core, m))
        greeted.append((z_hi * 32 + x_at * 8 + lax.rem(y_at + step, 4) * 2 + core, m))
    for other in greeted:
        pl.semaphore_signal(barrier, inc=1, device_id=other, device_id_type=MESH)
    own_frames = pltpu.make_async_copy(clip.at[pl.ds(m * 4, 4)], x, x_sem)
    own_frames.start()
    for k in range(6):
        load(k)
    pl.semaphore_wait(barrier, len(greeted))
    fetch_z(0)
    fetch_z(1)
    greet(0)
    perm[0] = one_hot(True)
    perm[1] = one_hot(False)
    own_frames.wait()

    @pl.loop(0, 4)
    def _(f):
        normed[pl.ds(pl.multiple_of(f * TOKENS, TOKENS), TOKENS)] = layer_norm(x[f], gain_s[...].reshape(1, D))

    columns = lax.broadcasted_iota(jnp.int32, (1, 3 * HALF), 1)
    scale = jnp.where(columns < HALF, Q_SCALE, 1.0).astype(F32)

    def spatial_qkv(half):
        @pl.loop(0, 4)
        def _(f):
            rows = pl.ds(pl.multiple_of(f * TOKENS, TOKENS), TOKENS)
            qkv_s[rows] = (dot(normed[rows], f0[half]) * scale).astype(BF16)

    def spatial_heads(half, f, start, count):
        rows = pl.ds(pl.multiple_of(f * TOKENS + start, count), count)
        every = pl.ds(pl.multiple_of(f * TOKENS, TOKENS), TOKENS)
        for pair in range(3):
            c = pair * 128
            mixed[rows, pl.ds(pl.multiple_of(half * HALF + c, 128), 128)] = attend_pair(
                qkv_s[rows, c : c + 128],
                qkv_s[every, HALF + c : HALF + c + 128],
                qkv_s[every, 2 * HALF + c : 2 * HALF + c + 128],
            )

    greet(1)
    spatial_qkv(m)
    fetch_ring(0)
    fetch_ring(1)
    fetch_z(2)
    fetch_z(3)
    greet(2)

    @pl.loop(0, 4)
    def _(f):
        @pl.when(f == 2)
        def _():
            fetch_far(0)
            fetch_z(4)
            fetch_z(5)
            greet(4)

        @pl.when(f == 1)
        def _():
            greet(3)

        @pl.when(f == 3)
        def _():
            greet(5)

        spatial_heads(m, f, 0, TOKENS)

    fetch_last(0)
    fetch_far(1)
    fetch_ring(2)
    greet(6)
    fetched(0)
    spatial_qkv(1 - m)
    fetch_last(1)
    fetch_ring(3)
    greet(7)

    @pl.loop(0, 2)
    def _(p):
        @pl.when(p == 1)
        def _():
            fetch_last(2)
            fetch_last(3)
            fetch_ring(4)
            fetch_ring(5)

        @pl.loop(0, 4)
        def _(f):
            @pl.when(jnp.logical_and(p == 0, f == 2))
            def _():
                fetch_far(2)
                fetch_far(3)

            spatial_heads(1 - m, f, p * 128, 128)

        @pl.when(p == 0)
        def _():
            fetched(1)

        patches = pl.ds(pl.multiple_of(p * 128, 128), 128)

        @pl.loop(0, 2)
        def _(pair):
            rows = [pl.ds(pl.multiple_of((pair * 2 + i) * TOKENS + p * 128, 128), 128) for i in range(2)]
            total = dot(jnp.concatenate([mixed[r] for r in rows], axis=0), f1[...])
            for i in range(2):
                f = pair * 2 + i
                x[f, patches] = (x[f, patches].astype(F32) + total[i * 128 : (i + 1) * 128]).astype(BF16)

        @pl.loop(0, 4)
        def _(b):
            to = lax.rem(group + b, 4)
            tokens = [
                x[f, pl.ds(pl.multiple_of(p * 128 + u * CHIPS + to * GROUP, GROUP), GROUP)]
                for u in range(2)
                for f in range(4)
            ]
            put(p, b, to, jnp.concatenate(tokens, axis=0), (0, 1), send1, recv1, a_send, a_recv)

    fetched(2)

    def hand_on_a(p):
        @pl.loop(0, 4)
        def _(b):
            hand_on(p, lax.rem(group + 4 - b, 4), recv1, a_recv, cross1, c_send, c_recv)

    def hand_on_b(p):
        @pl.loop(0, 4)
        def _(b):
            hand_on(p, lax.rem(group + b, 4), recv2, b_recv, cross2, d_send, d_recv)

    hand_on_a(0)

    @pl.loop(0, 2)
    def _(p):
        @pl.loop(0, 2)
        def _(pair):
            rows = pl.ds(pl.multiple_of(p * 512 + pair * TOKENS, TOKENS), TOKENS)
            tokens = jnp.concatenate(
                [take(p, lax.rem(group + 4 - pair * 2 - i, 4), recv1, cross1, c_recv) for i in range(2)], axis=0
            )
            positions[rows] = tokens
            normal = layer_norm(tokens, gain_t[...].reshape(1, D))
            for half in range(2):
                qkv_t[half, rows] = (dot(normal, f2[half]) * scale).astype(BF16)

        @pl.loop(0, 4)
        def _(t):
            @pl.when(jnp.logical_and(p == 0, t == 1))
            def _():
                fetch_far(4)
                fetch_far(5)

            @pl.when(jnp.logical_and(p == 0, t == 3))
            def _():
                fetch_last(4)
                fetch_last(5)

            half = t // 2
            every = pl.ds(pl.multiple_of(p * 512, 512), 512)
            rows = pl.ds(pl.multiple_of(p * 512 + lax.rem(t, 2) * TOKENS, TOKENS), TOKENS)
            for pair in range(3):
                c = pair * 128
                mixed[rows, pl.ds(pl.multiple_of(half * HALF + c, 128), 128)] = attend_pair(
                    qkv_t[half, rows, c : c + 128],
                    qkv_t[half, every, HALF + c : HALF + c + 128],
                    qkv_t[half, every, 2 * HALF + c : 2 * HALF + c + 128],
                )

        @pl.when(p == 0)
        def _():
            fetched(3)
            fetched(4)
            fetched(5)
            hand_on_a(1)

        @pl.when(p == 1)
        def _():
            hand_on_b(0)

        @pl.loop(0, 2)
        def _(pair):
            rows = pl.ds(pl.multiple_of(p * 512 + pair * TOKENS, TOKENS), TOKENS)
            tokens = (positions[rows].astype(F32) + dot(mixed[rows], f3[...])).astype(BF16)
            normal = layer_norm(tokens, gain_m[...].reshape(1, D))
            total = tokens.astype(F32)
            for j in range(4):
                up = dot(normal, f4[j // 2, :, (j % 2) * D : (j % 2 + 1) * D])
                total = total + dot(gelu(up).astype(BF16), f5[j * D : (j + 1) * D])
            done = total.astype(BF16)
            for i in range(2):
                b = pair * 2 + i
                to = lax.rem(group + 4 - b, 4)
                put(p, b, to, done[i * 128 : (i + 1) * 128], (core, 1 - core), send2, recv2, b_send, b_recv)

    hand_on_b(1)

    @pl.loop(0, 2)
    def _(p):
        @pl.loop(0, 4)
        def _(b):
            source = lax.rem(group + b, 4)
            tokens = take(p, source, recv2, cross2, d_recv)
            for u, of_core in enumerate((core, 1 - core)):
                rows = pl.ds(pl.multiple_of(p * 128 + of_core * CHIPS + source * GROUP, GROUP), GROUP)
                for f in range(4):
                    out[f, rows] = tokens[u * 64 + f * 16 : u * 64 + (f + 1) * 16]

    for p in range(2):
        for send, sem in ((send1, a_send), (send2, b_send)):
            landed(send.at[p, pl.ds(0, CHIPS - 1)], sem.at[p])
        for crossed, sem in ((cross1, c_send), (cross2, d_send)):
            landed(crossed.at[p], sem.at[p])
    for k in range(6):
        landed(part(k, 0, 0, ROWS[k] // 8), z_send.at[k])
        landed(part(k, 0, 0, ROWS[k] // 8 * 3), ring_send.at[k])
        landed(part(k, 0, 0, ROWS[k] // 2), core_send.at[k])


def per_device(clip, gain_s, gain_t, gain_m, w0, w1, w2, w3, w4, w5):
    w0, w2 = jnp.swapaxes(w0, 0, 1), jnp.swapaxes(w2, 0, 1)
    vmem, anywhere = pl.BlockSpec(memory_space=pltpu.VMEM), pl.BlockSpec(memory_space=pl.ANY)
    dma = pltpu.SemaphoreType.DMA
    return pl.pallas_call(
        kernel,
        out_shape=jax.ShapeDtypeStruct((4, 256, D), BF16),
        in_specs=[anywhere, vmem, vmem, vmem] + [anywhere] * 6,
        out_specs=vmem,
        scratch_shapes=[
            pltpu.VMEM((4, 256, D), BF16),
            pltpu.VMEM((1024, D), BF16),
            pltpu.VMEM((1024, 3 * HALF), BF16),
            pltpu.VMEM((2, 1024, 3 * HALF), BF16),
            pltpu.VMEM((1024, D), BF16),
            pltpu.VMEM((1024, D), BF16),
            pltpu.VMEM((2, CHIPS, 2, 24, 128), BF16),
            pltpu.VMEM((2, CHIPS, 2, 24, 128), BF16),
            pltpu.VMEM((2, CHIPS, 2, 24, 128), BF16),
            pltpu.VMEM((2, CHIPS, 2, 24, 128), BF16),
            pltpu.VMEM((2, CHIPS, 24, 128), BF16),
            pltpu.VMEM((2, CHIPS, 24, 128), BF16),
            pltpu.VMEM((2, PACKED, PACKED), BF16),
            pltpu.VMEM((2, D, 3 * HALF), BF16),
            pltpu.VMEM((D, D), BF16),
            pltpu.VMEM((2, D, 3 * HALF), BF16),
            pltpu.VMEM((D, D), BF16),
            pltpu.VMEM((2, D, 1536), BF16),
            pltpu.VMEM((3072, D), BF16),
            dma,
            dma((6,)),
            dma((6,)),
            dma((6, 2)),
            dma((6,)),
            dma((6, 2)),
            dma((6, 2)),
            dma((6,)),
            dma((6,)),
            pltpu.SemaphoreType.REGULAR((7,)),
            dma((2,)),
            dma((2, 4)),
            dma((2,)),
            dma((2, 4)),
            dma((2,)),
            dma((2, 4)),
            dma((2,)),
            dma((2, 4)),
        ],
        compiler_params=pltpu.CompilerParams(
            collective_id=0, has_side_effects=True, vmem_limit_bytes=60 << 20
        ),
        cost_estimate=pl.CostEstimate(
            flops=22 * 10**9, bytes_accessed=13 * 10**6, transcendentals=12 * 10**6
        ),
    )(clip, gain_s, gain_t, gain_m, w0, w1, w2, w3, w4, w5)


def solution(mesh):
    return jax.shard_map(
        per_device,
        mesh=mesh,
        in_specs=(
            P("seq", None, None),
            P(),
            P(),
            P(),
            P(None, None, "mp"),
            P("mp", None),
            P(None, None, "mp"),
            P("mp", None),
            P(None, "mp"),
            P("mp", None),
        ),
        out_specs=P(("seq", "mp"), None, None),
        check_vma=False,
    )
```
